32 devices in a mesh: groups: 2 (over x), slab: 16 (over z, y, core).
Axes of the slice: x: 2, y: 2, z: 4, core: 2. Of those that a mesh axis runs over, the one named last changes fastest.
Arguments:
- order_field: float32 [2, 216, 8192], P(None, None, ('groups', 'slab')), parts along dimension 2, may hold values from -6 to 6
- pinning: float32 [216, 8192], P(None, ('groups', 'slab')), parts along dimension 1, may hold values from -1 to 3
- metric: float32 [8192], P(('groups', 'slab')), parts along dimension 0, may hold values from 1 to 2
- elem_count: int32 [32], P(('groups', 'slab')), parts along dimension 0, may hold values from 128 to 256, as said below
- mortar_table: int32 [6, 49152], P(None, ('groups', 'slab')), parts along dimension 1, may hold values from -1 to 1535, as said below
Outputs:
- evolved: float32 [2, 216, 8192], P(None, None, ('groups', 'slab')), parts along dimension 2
The draws below stay inside these ranges and needn't reach their ends.
There are 2 independent parts, one for each index of `groups`. The reference program is written for one: setup_inputs(seed, part) draws one part's arguments, and reference() takes and returns one part's arrays. A program takes and returns all parts, laid end to end along the dimension named above; each array names one. Nothing has to cross between parts.
Inputs may be any that keep to these rules, and one draw needn't show every extreme that they name: `elem_count`: 256 is reached on some device in every draw. `mortar_table`: row 0 names a live element slot of the entry's device, row 1 a face 0 to 5, row 2 a subface 0 to 3 or 4 for the whole face (when one side of a pair has a subface under 4 the other has 4), row 3 an orientation 0 to 7, row 4 the partner's device (-1 for unused entries, the own device for pairs within it, else a device at most 2 away along slab), row 5 the partner's index on the own device, or for other devices a slot 0 to 127 equal on both sides and distinct among the entries between two devices. Entries of one device with one partner device number at most 128; some pair of devices reaches it in every draw. Pairs are matched both ways.
All inputs are finite; a program needn't handle non-finite values.
Results may differ from the reference program's by a relative error of at most 0.0003.
Values sent between devices are 32-bit elements; how exact they have to be, the bound alone decides.
No kernel may reach another device: no remote copies, remote signals or barrier semaphores. Data moves between devices by JAX's collectives and lax.ppermute only.
A program may use at most 64 MiB of HBM per device.

```python
import math
import jax
import jax.numpy as jnp
import numpy as np
from jax import lax

NODES = 216
E_DEV = 256
CAP = 128
REACH = 2
H_DEV = 1536
ELEMS = 4096
N_SLAB = 16


def random_perms(key, rows_total, length):
    return jax.vmap(lambda sub_key: jax.random.permutation(sub_key, length))(jax.random.split(key, rows_total)).astype(jnp.int32)


def side_fields(key, shape, owner_counts):
    subkeys = jax.random.split(key, 3)
    element = jax.random.randint(subkeys[0], shape, 0, owner_counts[:, None])
    face_no = jax.random.randint(subkeys[1], shape, 0, 6)
    orient = jax.random.randint(subkeys[2], shape, 0, 8)
    return (element, face_no, orient)


def masked_fields(alive, values):
    defaults = (0, 0, 4, 0, -1, 0)
    return tuple((jnp.where(alive, value_now, default_now).astype(jnp.int32) for value_now, default_now in zip(values, defaults)))


def mesh_tables(key):
    devices = N_SLAB
    capacity = CAP
    local_len = H_DEV - 2 * REACH * capacity
    pair_slots = local_len // 2
    subkeys = jax.random.split(key, 16)
    counts = jax.random.randint(subkeys[0], (devices,), E_DEV // 2, E_DEV + 1)
    fullest = jax.random.randint(subkeys[1], (), 0, devices)
    device_rows = jnp.arange(devices, dtype=jnp.int32)
    counts = jnp.where(device_rows == fullest, E_DEV, counts).astype(jnp.int32)
    position = random_perms(subkeys[2], devices, H_DEV)
    row_column = device_rows[:, None]
    tables = tuple((jnp.full((devices, H_DEV), fill_value, jnp.int32) for fill_value in (0, 0, 4, 0, -1, 0)))

    def place_into(current, spots, values):
        return tuple((table_now.at[row_column, spots].set(value_now) for table_now, value_now in zip(current, values)))
    pair_count = jax.random.randint(subkeys[3], (devices,), local_len // 4, local_len // 2 + 1)
    pair_index = jnp.arange(pair_slots, dtype=jnp.int32)[None, :]
    pair_live = pair_index < pair_count[:, None]
    spot_a = jnp.take_along_axis(position, jnp.broadcast_to(2 * pair_index, (devices, pair_slots)), axis=1)
    spot_b = jnp.take_along_axis(position, jnp.broadcast_to(2 * pair_index + 1, (devices, pair_slots)), axis=1)
    elem_a, face_a, orient_a = side_fields(subkeys[4], (devices, pair_slots), counts)
    elem_b, face_b, orient_b = side_fields(subkeys[5], (devices, pair_slots), counts)
    pair_kind = jax.random.randint(subkeys[6], (devices, pair_slots), 0, 4)
    quarter = jax.random.randint(subkeys[7], (devices, pair_slots), 0, 4)
    sub_a = jnp.where(pair_kind == 2, quarter, 4)
    sub_b = jnp.where(pair_kind == 3, quarter, 4)
    tables = place_into(tables, spot_a, masked_fields(pair_live, (elem_a, face_a, sub_a, orient_a, row_column + 0 * spot_a, spot_b)))
    tables = place_into(tables, spot_b, masked_fields(pair_live, (elem_b, face_b, sub_b, orient_b, row_column + 0 * spot_b, spot_a)))
    for reach_no in range(1, REACH + 1):
        reach_keys = jax.random.split(subkeys[7 + reach_no], 10)
        target_ok = device_rows + reach_no < devices
        load = jax.random.randint(reach_keys[0], (devices,), max(1, capacity // 3), capacity + 1)
        if reach_no == 1:
            full_pair = jax.random.randint(reach_keys[1], (), 0, devices - 1)
            load = jnp.where(device_rows == full_pair, capacity, load)
        load = jnp.where(target_ok, load, 0)
        slot_index = jnp.arange(capacity, dtype=jnp.int32)[None, :]
        live_a = slot_index < load[:, None]
        wire = random_perms(reach_keys[2], devices, capacity)
        side_a = random_perms(reach_keys[3], devices, capacity)
        side_b = random_perms(reach_keys[4], devices, capacity)
        pair_kind = jax.random.randint(reach_keys[5], (devices, capacity), 0, 4)
        quarter = jax.random.randint(reach_keys[6], (devices, capacity), 0, 4)
        base_up = local_len + (reach_no - 1) * capacity
        base_down = local_len + (REACH + reach_no - 1) * capacity
        elem_a, face_a, orient_a = side_fields(reach_keys[7], (devices, capacity), counts)
        spot_a = jnp.take_along_axis(position, base_up + side_a, axis=1)
        sub_a = jnp.where(pair_kind == 2, quarter, 4)
        tables = place_into(tables, spot_a, masked_fields(live_a, (elem_a, face_a, sub_a, orient_a, row_column + reach_no + 0 * wire, wire)))
        live_b = jnp.roll(live_a, reach_no, axis=0) & (row_column >= reach_no)
        wire_b = jnp.roll(wire, reach_no, axis=0)
        sub_b = jnp.roll(jnp.where(pair_kind == 3, quarter, 4), reach_no, axis=0)
        spot_b = jnp.take_along_axis(position, base_down + jnp.roll(side_b, reach_no, axis=0), axis=1)
        elem_b, face_b, orient_b = side_fields(reach_keys[8], (devices, capacity), counts)
        tables = place_into(tables, spot_b, masked_fields(live_b, (elem_b, face_b, sub_b, orient_b, row_column - reach_no + 0 * wire_b, wire_b)))
    stacked = jnp.stack(tables).reshape(6, devices * H_DEV)
    return (counts, stacked)


def draw_elem_count(key, part):
    shared = mesh_tables(key)
    key = jax.random.fold_in(key, 1)
    return shared[0]


def draw_mortar_table(key, part):
    shared = mesh_tables(key)
    key = jax.random.fold_in(key, 2)
    return shared[1]


def level_of(own_key, dims, shards, smallest, largest):
    level = 1.0
    for axis_at, parts in shards:
        heights = jax.random.uniform(jax.random.fold_in(jax.random.fold_in(own_key, 6), axis_at), (parts,), jnp.float32, smallest / len(shards), largest / len(shards))
        level = level * jnp.repeat(jnp.exp(heights), dims[axis_at] // parts).reshape((-1,) + (1,) * (len(dims) - 1 - axis_at))
    return level


def gaussian(key, shape, width, reach, cuts=(), held_as=jnp.bfloat16):
    factor_of = level_of(key, shape, cuts, -0.22, 0.18) if cuts else 1.0
    entries = jax.random.normal(key, shape, jnp.float32) * width * factor_of
    return jnp.minimum(jnp.maximum(entries, -reach), reach).astype(held_as)


def setup_inputs(seed: int = 0, part: int = 0) -> dict:
    seeds = jax.random.split(jax.random.key(seed), 6)
    part_keys = jax.random.split(jax.random.fold_in(seeds[5], part), 6)
    order_field = gaussian(part_keys[0], (2, NODES, ELEMS), 1.0, 6.0, ((2, 16),), jnp.float32)
    pinning = jnp.clip(-1.0 + 4.0 * jax.random.uniform(part_keys[1], (NODES, ELEMS), jnp.float32) ** level_of(part_keys[1], (NODES, ELEMS), ((1, 16),), -0.2, 0.2), -1.0, 3.0)
    metric = jnp.clip(jnp.exp(math.log(2.0) - 0.6931472 * jax.random.uniform(part_keys[2], (ELEMS,), jnp.float32) ** level_of(part_keys[2], (ELEMS,), ((0, 16),), -0.2, 0.2)), 1.0, 2.0)
    elem_count = draw_elem_count(jax.random.fold_in(jax.random.fold_in(seeds[5], part), 71), part)
    mortar_table = draw_mortar_table(jax.random.fold_in(jax.random.fold_in(seeds[5], part), 71), part)
    return dict(order_field=order_field, pinning=pinning, metric=metric, elem_count=elem_count, mortar_table=mortar_table)


PENALTY = 18.0
LIFTING = 15.0
DIFFUSION = 0.001
TIME_STEP = 0.1
HIGHEST = lax.Precision.HIGHEST

def gll_points():
    inner_pt = np.sqrt(1.0 / 3.0 - 2.0 * np.sqrt(7.0) / 21.0)
    outer_pt = np.sqrt(1.0 / 3.0 + 2.0 * np.sqrt(7.0) / 21.0)
    return np.array([-1.0, -outer_pt, -inner_pt, inner_pt, outer_pt, 1.0])

def gll_weights(points):
    legendre = (63.0 * points ** 5 - 70.0 * points ** 3 + 15.0 * points) / 8.0
    return 2.0 / (30.0 * legendre ** 2)

def lagrange_matrix(points, targets):
    result = np.ones((targets.shape[0], points.shape[0]))
    for column in range(points.shape[0]):
        for other in range(points.shape[0]):
            if other != column:
                result[:, column] *= (targets - points[other]) / (points[column] - points[other])
    return result

def deriv_matrix(points):
    npoints = points.shape[0]
    factor = np.array([np.prod([points[one] - points[other] for other in range(npoints) if other != one]) for one in range(npoints)])
    result = np.zeros((npoints, npoints))
    for row_no in range(npoints):
        for col_no in range(npoints):
            if row_no != col_no:
                result[row_no, col_no] = factor[row_no] / (factor[col_no] * (points[row_no] - points[col_no]))
        result[row_no, row_no] = -np.sum(result[row_no])
    return result

def second_matrix():
    derivative = deriv_matrix(gll_points())
    return np.array([[np.sum(derivative[row_no, :] * derivative[:, col_no]) for col_no in range(6)] for row_no in range(6)])

def node_at(direction, along_idx, first_idx, second_idx):
    if direction == 0:
        return 36 * along_idx + 6 * first_idx + second_idx
    if direction == 1:
        return 36 * first_idx + 6 * along_idx + second_idx
    return 36 * first_idx + 6 * second_idx + along_idx

def face_tables():
    derivative = deriv_matrix(gll_points())
    face_nodes = np.zeros((6, 36), np.int32)
    face_rows = np.zeros((6, 2, 36, 216))
    for face_no in range(6):
        direction = face_no // 2
        end_index = 5 * (face_no % 2)
        normal_sign = 1.0 if face_no % 2 else -1.0
        for first_idx in range(6):
            for second_idx in range(6):
                face_slot = first_idx * 6 + second_idx
                face_node = node_at(direction, end_index, first_idx, second_idx)
                face_nodes[face_no, face_slot] = face_node
                face_rows[face_no, 0, face_slot, face_node] = 1.0
                for along_idx in range(6):
                    face_rows[face_no, 1, face_slot, node_at(direction, along_idx, first_idx, second_idx)] += normal_sign * derivative[end_index, along_idx]
    return (face_nodes, face_rows)

def mortar_tables():
    points = gll_points()
    weights = gll_weights(points)
    halves = [lagrange_matrix(points, (points - 1.0) / 2.0), lagrange_matrix(points, (points + 1.0) / 2.0)]
    face_weight = np.outer(weights, weights).reshape(36)
    to_mortar = np.stack([np.kron(halves[quarter // 2], halves[quarter % 2]) for quarter in range(4)])
    to_face = np.stack([0.25 * to_mortar[quarter].T * face_weight[None, :] / face_weight[:, None] for quarter in range(4)])
    return (to_mortar, to_face)

def orient_tables():
    source = np.zeros((8, 36), np.int32)
    for orient_code in range(8):
        for first_idx in range(6):
            for second_idx in range(6):
                first_src = 5 - first_idx if orient_code & 1 else first_idx
                second_src = 5 - second_idx if orient_code & 2 else second_idx
                if orient_code & 4:
                    first_src, second_src = (second_src, first_src)
                source[orient_code, first_idx * 6 + second_idx] = first_src * 6 + second_src
    return (source, np.argsort(source, axis=1).astype(np.int32))

def element_laplacian(field):
    second = jnp.asarray(second_matrix(), jnp.float32)
    elems = field.shape[2]
    cube = field.reshape(2, 6, 6, 6, elems)
    result = jnp.einsum('ai,cijke->cajke', second, cube, precision=HIGHEST)
    result = result + jnp.einsum('aj,cijke->ciake', second, cube, precision=HIGHEST)
    result = result + jnp.einsum('ak,cijke->cijae', second, cube, precision=HIGHEST)
    return result.reshape(2, 216, elems)

def mortar_traces(field, metric, table):
    face_nodes, face_rows = face_tables()
    to_mortar, to_face = mortar_tables()
    source, inverse = orient_tables()
    elems = field.shape[2]
    element, face_no, subface, orient = (table[0], table[1], table[2], table[3])
    face_values = jnp.einsum('pn,cne->pce', jnp.asarray(face_rows.reshape(432, 216), jnp.float32), field, precision=HIGHEST)
    face_values = face_values.reshape(6, 2, 36, 2, elems).transpose(1, 3, 2, 0, 4).reshape(144, 6 * elems)
    picked = jnp.take(face_values, face_no * elems + element, axis=1).reshape(2, 2, 36, -1)
    own_metric = jnp.take(metric, element)
    picked = jnp.stack([picked[0], picked[1] * own_metric])
    projected = jnp.where(subface == 4, picked, 0.0)
    for quarter in range(4):
        mortar_part = jnp.einsum('mn,kcnh->kcmh', jnp.asarray(to_mortar[quarter], jnp.float32), picked, precision=HIGHEST)
        projected = projected + jnp.where(subface == quarter, mortar_part, 0.0)
    node_index = jnp.asarray(source)[orient].T
    canonical = jnp.take_along_axis(projected, jnp.broadcast_to(node_index, projected.shape), axis=2)
    return jnp.concatenate([canonical.reshape(144, -1), own_metric[None, :]], axis=0)

def mortar_correction(own_trace, partner_trace):
    own_part = own_trace[:144].reshape(2, 2, 36, -1)
    partner_part = partner_trace[:144].reshape(2, 2, 36, -1)
    penalty_w = PENALTY * 0.5 * (own_trace[144] + partner_trace[144])
    return penalty_w * (partner_part[0] - own_part[0]) - 0.5 * (own_part[1] + partner_part[1])

def element_rate(field, pinning, metric, table, correction):
    face_nodes, face_rows = face_tables()
    to_mortar, to_face = mortar_tables()
    source, inverse = orient_tables()
    elems = field.shape[2]
    element, face_no, subface, orient = (table[0], table[1], table[2], table[3])
    correction = jnp.where(table[4] >= 0, correction, 0.0)
    node_index = jnp.asarray(inverse)[orient].T
    restored = jnp.take_along_axis(correction, jnp.broadcast_to(node_index, correction.shape), axis=1)
    on_face = jnp.where(subface == 4, restored, 0.0)
    for quarter in range(4):
        face_part = jnp.einsum('mn,cnh->cmh', jnp.asarray(to_face[quarter], jnp.float32), restored, precision=HIGHEST)
        on_face = on_face + jnp.where(subface == quarter, face_part, 0.0)
    on_face = on_face * (LIFTING * jnp.take(metric, element))
    columns = (jnp.asarray(face_nodes)[face_no].T * elems + element[None, :]).reshape(-1)
    lifted = jnp.zeros((2, 216 * elems), jnp.float32).at[:, columns].add(on_face.reshape(2, -1)).reshape(2, 216, elems)
    return DIFFUSION * (metric * metric * element_laplacian(field) + lifted) - pinning * field

def section_rate(field, pinning, metric, mortar_table):
    devices = N_SLAB
    offsets = [shift_by for shift_by in range(-REACH, REACH + 1) if shift_by != 0]
    per_field = field.reshape(2, 216, devices, E_DEV).transpose(2, 0, 1, 3)
    per_pin = pinning.reshape(216, devices, E_DEV).transpose(1, 0, 2)
    per_metric = metric.reshape(devices, E_DEV)
    per_table = mortar_table.reshape(6, devices, H_DEV).transpose(1, 0, 2)
    device_ids = jnp.arange(devices, dtype=jnp.int32)

    def outgoing(inputs):
        own_id, own_field, own_metric, own_table = inputs
        traces = mortar_traces(own_field, own_metric, own_table)
        buffers = []
        for shift_by in offsets:
            chosen = own_table[4] == own_id + shift_by
            slot_cols = jnp.where(chosen, own_table[5], CAP)
            buffers.append(jnp.zeros((145, CAP), jnp.float32).at[:, slot_cols].set(traces, mode='drop'))
        return jnp.stack(buffers)
    outgoing_all = lax.map(outgoing, (device_ids, per_field, per_metric, per_table))

    def update(inputs):
        own_id, own_field, own_pin, own_metric, own_table = inputs
        traces = mortar_traces(own_field, own_metric, own_table)
        received = []
        for place_no, shift_by in enumerate(offsets):
            sender = own_id - shift_by
            in_range = (sender >= 0) & (sender < devices)
            piece_in = lax.dynamic_index_in_dim(outgoing_all, jnp.clip(sender, 0, devices - 1), 0, keepdims=False)[place_no]
            received.append(jnp.where(in_range, piece_in, 0.0))
        inbound = jnp.concatenate(received, axis=1)
        partner_dev = own_table[4]
        link_slot = own_table[5]
        distance = own_id - partner_dev
        place_idx = jnp.where(distance < 0, distance + REACH, distance + REACH - 1)
        remote_col = jnp.clip(place_idx, 0, 2 * REACH - 1) * CAP + jnp.clip(link_slot, 0, CAP - 1)
        local_col = jnp.clip(link_slot, 0, H_DEV - 1)
        partner = jnp.where(partner_dev == own_id, jnp.take(traces, local_col, axis=1), jnp.take(inbound, remote_col, axis=1))
        correction = mortar_correction(traces, partner)
        return element_rate(own_field, own_pin, own_metric, own_table, correction)
    all_rates = lax.map(update, (device_ids, per_field, per_pin, per_metric, per_table))
    return all_rates.transpose(1, 2, 0, 3).reshape(2, 216, devices * E_DEV)

def reference(order_field, pinning, metric, elem_count, mortar_table):
    alive = jnp.arange(E_DEV, dtype=jnp.int32)[None, :] < elem_count[:, None]
    initial = jnp.where(alive.reshape(-1), order_field, 0.0)
    first_section = initial + TIME_STEP * section_rate(initial, pinning, metric, mortar_table)
    second_section = first_section + TIME_STEP * section_rate(first_section, pinning, metric, mortar_table)
    return 0.5 * initial + 0.5 * second_section
```

```python
import functools

import jax
import jax.numpy as jnp
import numpy as np
from jax import lax
from jax.experimental import pallas as pl
from jax.experimental.pallas import tpu as pltpu
from jax.sharding import PartitionSpec as P

CAP = 128
CHANNELS = 4
PENALTY = 18.0
LIFTING = 15.0
DIFFUSION = 0.001
TIME_STEP = 0.1
F32 = jnp.float32
BF16 = jnp.bfloat16
I32 = jnp.int32


def gll_points():
    inner_pt = np.sqrt(1.0 / 3.0 - 2.0 * np.sqrt(7.0) / 21.0)
    outer_pt = np.sqrt(1.0 / 3.0 + 2.0 * np.sqrt(7.0) / 21.0)
    return np.array([-1.0, -outer_pt, -inner_pt, inner_pt, outer_pt, 1.0])


def gll_weights(points):
    legendre = (63.0 * points**5 - 70.0 * points**3 + 15.0 * points) / 8.0
    return 2.0 / (30.0 * legendre**2)


def lagrange_matrix(points, targets):
    result = np.ones((targets.shape[0], points.shape[0]))
    for column in range(points.shape[0]):
        for other in range(points.shape[0]):
            if other != column:
                result[:, column] *= (targets - points[other]) / (points[column] - points[other])
    return result


def deriv_matrix(points):
    npoints = points.shape[0]
    factor = np.array(
        [
            np.prod([points[one] - points[other] for other in range(npoints) if other != one])
            for one in range(npoints)
        ]
    )
    result = np.zeros((npoints, npoints))
    for row_no in range(npoints):
        for col_no in range(npoints):
            if row_no != col_no:
                result[row_no, col_no] = factor[row_no] / (
                    factor[col_no] * (points[row_no] - points[col_no])
                )
        result[row_no, row_no] = -np.sum(result[row_no])
    return result


def second_matrix():
    derivative = deriv_matrix(gll_points())
    return np.array(
        [
            [np.sum(derivative[row_no, :] * derivative[:, col_no]) for col_no in range(6)]
            for row_no in range(6)
        ]
    )


def node_at(direction, along_idx, first_idx, second_idx):
    if direction == 0:
        return 36 * along_idx + 6 * first_idx + second_idx
    if direction == 1:
        return 36 * first_idx + 6 * along_idx + second_idx
    return 36 * first_idx + 6 * second_idx + along_idx


PAD = 40


def split_np(matrix):
    whole = np.asarray(matrix, np.float32)
    high = whole.astype(BF16)
    return high, (whole - high.astype(np.float32)).astype(BF16)


def constant_tables():
    points = gll_points()
    weights = gll_weights(points)
    derivative = deriv_matrix(points)
    second = second_matrix()
    lap = np.zeros((216, 216))
    for i in range(6):
        for j in range(6):
            for k in range(6):
                row = 36 * i + 6 * j + k
                for m in range(6):
                    lap[row, 36 * m + 6 * j + k] += second[i, m]
                    lap[row, 36 * i + 6 * m + k] += second[j, m]
                    lap[row, 36 * i + 6 * j + m] += second[k, m]
    value = np.zeros((6 * PAD, 216))
    normal = np.zeros((6 * PAD, 216))
    for face in range(6):
        direction, end = face // 2, 5 * (face % 2)
        sign = 1.0 if face % 2 else -1.0
        for a in range(6):
            for b in range(6):
                row = face * PAD + 6 * a + b
                value[row, node_at(direction, end, a, b)] = 1.0
                for m in range(6):
                    normal[row, node_at(direction, m, a, b)] += sign * derivative[end, m]
    to_half = [
        lagrange_matrix(points, (points - 1.0) / 2.0),
        lagrange_matrix(points, (points + 1.0) / 2.0),
    ]
    from_half = [0.5 * half.T * weights[None, :] / weights[:, None] for half in to_half]
    own = [from_half[side] @ to_half[side] for side in range(2)]
    place = value.T
    blocks = []
    for quarter in range(4):
        both = np.zeros((PAD, PAD))
        both[:36, :36] = np.kron(own[quarter // 2], own[quarter % 2])
        blocks.append(place @ np.kron(np.eye(6), both))
    blocks.append(place)
    own_place = np.concatenate(blocks, axis=1)
    return dict(
        lap=split_np(lap),
        value=value.astype(BF16),
        normal=split_np(normal),
        own=split_np(own_place),
        place=place.astype(BF16),
        to_half=to_half,
        from_half=from_half,
    )


TABLES = constant_tables()


def split(x):
    high = x.astype(BF16)
    return high, (x - high.astype(F32)).astype(BF16)


def mm(a, b):
    return jnp.dot(a, b, preferred_element_type=F32)


def mm_nt(a, b):
    return lax.dot_general(a, b, (((1,), (1,)), ((), ())), preferred_element_type=F32)


def mm3(const_high, const_low, x):
    high, low = split(x)
    return mm(const_high, high) + mm(const_high, low) + mm(const_low, high)


def sub_iota(shape):
    return lax.broadcasted_iota(I32, shape, 0)


def one_hot(row, length):
    return jnp.where(sub_iota((length, row.shape[1])) == row, 1.0, 0.0).astype(BF16)


def as_int(row):
    return row.astype(I32)


def stack_rows(rows, lanes):
    at = sub_iota((8, lanes))
    out = jnp.zeros((8, lanes), F32)
    for place, row in enumerate(rows):
        out = jnp.where(at == place, row, out)
    return out


def face_tables_of(u, metric2, value, normal_high, normal_low, table_ref):
    elems = u.shape[1] // 2
    high, low = split(u)
    v_parts = (mm(value, high).astype(BF16), mm(value, low).astype(BF16))
    g = (mm(normal_high, high) + mm(normal_high, low) + mm(normal_low, high)) * metric2
    g_parts = split(g)
    rows = 6 * PAD
    for part in range(2):
        for kind, parts in enumerate((v_parts, g_parts)):
            for comp in range(2):
                at = ((part * 2 + kind) * 2 + comp) * rows
                table_ref[at : at + rows, :] = parts[part][:, comp * elems : (comp + 1) * elems]


def gather_faces(table_ref, elem_row, face_row, out_ref):
    elems = table_ref.shape[1]
    rows = 6 * PAD
    lanes = elem_row.shape[1]
    step = 256
    for start in range(0, lanes, step):
        hot = one_hot(elem_row[:, start : start + step], elems)
        got = mm(table_ref[...], hot)
        face = face_row[:, start : start + step]
        for kind in range(2):
            for comp in range(2):
                at = (kind * 2 + comp) * rows
                low_at = at + 4 * rows
                picked = got[at : at + PAD] + got[low_at : low_at + PAD]
                for f in range(1, 6):
                    mine = (
                        got[at + f * PAD : at + (f + 1) * PAD]
                        + got[low_at + f * PAD : low_at + (f + 1) * PAD]
                    )
                    picked = jnp.where(face == f, mine, picked)
                for t in range(step // 128):
                    tile = start // 128 + t
                    to = (2 * tile + comp) * 2 * PAD + kind * PAD
                    out_ref[to : to + PAD, :] = picked[:, t * 128 : (t + 1) * 128]


def spread(att, ref):
    tiles = att.shape[1] // 128
    for tile in range(tiles):
        for comp in range(2):
            at = (2 * tile + comp) * 8
            ref[at : at + 8, :] = att[:, tile * 128 : (tile + 1) * 128]

    def get(row):
        return ref[pl.ds(row, 2 * tiles, stride=8), :]

    return get


def axis_classes(quarter, orient):
    swap = (orient & 4) > 0
    first = quarter // 2
    second = quarter - 2 * first
    whole = quarter == 4
    a = jnp.where(whole, 2, jnp.where(swap, second, first))
    b = jnp.where(whole, 2, jnp.where(swap, first, second))
    return swap, a, b, (orient & 1) > 0, (orient & 2) > 0


def axis_matrix(cls, flip, halves, flip_rows):
    out = {}
    is0, is1 = cls == 0, cls == 1
    for r in range(6):
        for c in range(6):

            def entry(r0, c0):
                return jnp.where(
                    is0,
                    float(halves[0][r0, c0]),
                    jnp.where(is1, float(halves[1][r0, c0]), 1.0 if r0 == c0 else 0.0),
                )

            flipped = entry(5 - r, c) if flip_rows else entry(r, 5 - c)
            out[r, c] = jnp.where(flip, flipped, entry(r, c))
    return out


def source_matrices(quarter, orient):
    swap, a, b, flip_a, flip_b = axis_classes(quarter, orient)
    halves = TABLES["to_half"]
    return swap, axis_matrix(a, flip_a, halves, True), axis_matrix(b, flip_b, halves, True)


def target_matrices(quarter, orient):
    swap, a, b, flip_a, flip_b = axis_classes(quarter, orient)
    halves = TABLES["from_half"]
    return swap, axis_matrix(a, flip_a, halves, False), axis_matrix(b, flip_b, halves, False)


def put_matrices(ref, a, b, swap):
    for r in range(6):
        for c in range(6):
            ref[6 * r + c] = a[r, c]
            ref[36 + 6 * r + c] = b[r, c]
    ref[72] = jnp.where(swap, 1.0, 0.0)


def two_axes(x, coef, rows):
    y = {}
    for b in range(6):
        for r in range(6):
            acc = coef[6 * r, rows] * x[0, b]
            for a in range(1, 6):
                acc = acc + coef[6 * r + a, rows] * x[a, b]
            y[r, b] = acc
    z = {}
    for r in range(6):
        for s in range(6):
            acc = coef[36 + 6 * s, rows] * y[r, 0]
            for b in range(1, 6):
                acc = acc + coef[36 + 6 * s + b, rows] * y[r, b]
            z[r, s] = acc
    return z


def swapped(x, swap):
    return {
        (a, b): x[a, b] if a == b else jnp.where(swap, x[b, a], x[a, b])
        for a in range(6)
        for b in range(6)
    }


def scatter_faces(z_ref, elem_row, face_row, elems, left_ref):
    lanes = elem_row.shape[1]
    width = 6 * 2 * PAD
    for tile in range(lanes // 128):
        at = slice(tile * 128, (tile + 1) * 128)
        high, low = split(z_ref[tile * 2 * PAD : (tile + 1) * 2 * PAD, :])
        face = face_row[:, at]
        for f in range(6):
            mask = jnp.where(face == f, 1.0, 0.0).astype(BF16)
            left_ref[f * 2 * PAD : (f + 1) * 2 * PAD, at] = high * mask
            left_ref[width + f * 2 * PAD : width + (f + 1) * 2 * PAD, at] = low * mask
    hot = one_hot(elem_row, elems)
    both = mm_nt(left_ref[...], hot)
    return both[:width] + both[width:]


def side_by_side(sums, elems):
    out = []
    for f in range(6):
        at = f * 2 * PAD
        out.append(jnp.concatenate([sums[at : at + PAD], sums[at + PAD : at + 2 * PAD]], axis=1))
    return jnp.concatenate(out, axis=0)


def zero_pad_rows(ref, blocks):
    for block in range(blocks):
        ref[block * PAD + 32 : block * PAD + 40, :] = jnp.zeros((8, 128), F32)


def both_lanes(x):
    return jnp.concatenate([x, x], axis=1)


def send_message(table_ref, slot_rows, coef_ref, xs_ref, spread_ref, out_ref, first, mp=None):
    gather_faces(table_ref, as_int(slot_rows[0:1]), as_int(slot_rows[1:2]), xs_ref)
    get = spread(slot_rows, spread_ref)
    own_m = get(5)
    rows = slice(None)
    swap = coef_ref[72] > 0.5

    def load(kind):
        return {
            (a, b): xs_ref[pl.ds(kind * PAD + 6 * a + b, 2 * CHANNELS, stride=2 * PAD), :]
            for a in range(6)
            for b in range(6)
        }

    if first:
        v = two_axes(swapped(load(0), swap), coef_ref, rows)
        g = two_axes(swapped(load(1), swap), coef_ref, rows)
        stride = 2 * PAD + 8
        for a in range(6):
            for b in range(6):
                n = 6 * a + b
                out_ref[pl.ds(n, 8, stride=stride), :] = v[a, b]
                out_ref[pl.ds(PAD + n, 8, stride=stride), :] = (0.5 * PENALTY * own_m) * v[a, b] - 0.5 * g[a, b]
        for n in range(36, 40):
            out_ref[pl.ds(n, 8, stride=stride), :] = own_m
            out_ref[pl.ds(PAD + n, 8, stride=stride), :] = own_m
        for n in range(80, 88):
            out_ref[pl.ds(n, 8, stride=stride), :] = own_m
    else:
        tau = 0.5 * PENALTY * (own_m + mp)
        v, g = load(0), load(1)
        x = {key: tau * v[key] - 0.5 * g[key] for key in v}
        z = two_axes(swapped(x, swap), coef_ref, rows)
        for a in range(6):
            for b in range(6):
                out_ref[pl.ds(6 * a + b, 8, stride=PAD), :] = z[a, b]
        for n in range(36, 40):
            out_ref[pl.ds(n, 8, stride=PAD), :] = own_m


def prepare(
    own_ref, count_ref, field_ref, metric_ref, table_ref, value_ref, normal_high_ref, normal_low_ref,
    u_ref, faces_ref, entry_ref, partner_ref, slot_ref, counts_ref, coef_ref, msg_ref,
    xs_ref, spread_ref,
):
    elems = field_ref.shape[2]
    lanes = table_ref.shape[1]
    tiles = lanes // 128
    own = own_ref[0]
    alive = lax.broadcasted_iota(I32, (1, elems), 1) < count_ref[0]
    u = jnp.concatenate([jnp.where(alive, field_ref[comp], 0.0) for comp in range(2)], axis=1)
    u_ref[...] = u
    metric = metric_ref[...]
    face_tables_of(
        u, both_lanes(metric), value_ref[...], normal_high_ref[...], normal_low_ref[...], faces_ref
    )
    element, face, quarter, orient, partner, link = (table_ref[r : r + 1, :] for r in range(6))
    used = partner >= 0
    local = partner == own
    distance = partner - own
    near = 1 - 2 * (own & 1)
    far = 2 - 2 * (own & 2)
    channel = jnp.where(
        distance == near, 0, jnp.where(distance == -near, 1, jnp.where(distance == far, 2, 3))
    )
    channel = jnp.where(used & jnp.logical_not(local), channel, -1)
    m1 = metric.astype(BF16).astype(F32)
    m2 = (metric - m1).astype(BF16).astype(F32)
    m3 = metric - m1 - m2
    hot = one_hot(element, elems)
    metric_rows = mm(stack_rows([m1, m2, m3], elems).astype(BF16), hot)
    parts = [metric_rows[r : r + 1] for r in range(3)]
    att = stack_rows([element.astype(F32), face.astype(F32), quarter.astype(F32), orient.astype(F32),
                      jnp.where(used, 1.0, 0.0)] + parts, lanes)
    link_hot = one_hot(link & (CAP - 1), CAP)
    left = jnp.concatenate([jnp.where(channel == s, att, 0.0) for s in range(CHANNELS)], axis=0)
    slots = mm_nt(left.astype(BF16), link_hot)
    slots = jnp.concatenate([slots[8 * s : 8 * s + 8] for s in range(CHANNELS)], axis=1)

    def finished(rows8, n):
        total = rows8[5:6] + rows8[6:7] + rows8[7:8]
        return jnp.where(sub_iota((8, n)) == 5, total, rows8)

    slot_rows = finished(slots, CHANNELS * CAP)
    slot_ref[...] = slot_rows
    left = jnp.concatenate([att[:, t * 128 : (t + 1) * 128] for t in range(tiles)], axis=0)
    spots = mm(left.astype(BF16), link_hot)
    high_link = link // CAP
    mates = spots[0:8]
    for t in range(1, tiles):
        mates = jnp.where(high_link == t, spots[8 * t : 8 * t + 8], mates)
    mates = finished(mates, lanes)
    partner_ref[...] = mates
    entry = finished(att, lanes)
    entry = jnp.where((sub_iota((8, lanes)) == 4) & jnp.logical_not(local), 0.0, entry)
    entry_ref[...] = entry
    kinds = sub_iota((48, lanes)) == 8 * face + quarter
    counts_ref[0] = mm_nt(jnp.where(kinds & used, 1.0, 0.0).astype(BF16), hot)
    weight = jnp.where(kinds & local, mates[5:6], 0.0)
    high, low = split(weight)
    counts_ref[1] = mm_nt(high, hot) + mm_nt(low, hot)

    get = spread(slot_rows, spread_ref)
    swap, a, b = source_matrices(as_int(get(2)), as_int(get(3)))
    put_matrices(coef_ref, a, b, swap)
    send_message(faces_ref, slot_rows, coef_ref, xs_ref, spread_ref, msg_ref, True)


def local_entries(faces_ref, entry, mates, coef_ref, xs_ref, zs_ref, spread_ref, left_ref):
    lanes = entry.shape[1]
    tiles = lanes // 128
    elems = faces_ref.shape[1]
    gather_faces(faces_ref, as_int(mates[0:1]), as_int(mates[1:2]), xs_ref)
    own_m = spread(entry, spread_ref)(5)
    mate_m = spread(mates, spread_ref)(5)
    tau_all = 0.5 * PENALTY * (own_m + mate_m)
    zero_pad_rows(zs_ref, 2 * tiles)
    for group in range(2 * tiles // 8):
        rows = slice(8 * group, 8 * group + 8)
        base = 8 * group * 2 * PAD
        tau = tau_all[rows]
        swap = coef_ref[72, rows] > 0.5
        x = {}
        for a in range(6):
            for b in range(6):
                n = 6 * a + b
                v = xs_ref[pl.ds(base + n, 8, stride=2 * PAD), :]
                g = xs_ref[pl.ds(base + PAD + n, 8, stride=2 * PAD), :]
                x[a, b] = tau * v - 0.5 * g
        z = two_axes(swapped(x, swap), coef_ref, rows)
        for a in range(6):
            for b in range(6):
                zs_ref[pl.ds(8 * group * PAD + 6 * a + b, 8, stride=PAD), :] = z[a, b]
    face = jnp.where(entry[4:5] > 0.5, as_int(entry[1:2]), -1)
    return scatter_faces(zs_ref, as_int(entry[0:1]), face, elems, left_ref)


def local_first(
    faces_ref, entry_ref, partner_ref, slot_ref, metric_ref, u_ref, pin_ref, lap_high_ref, lap_low_ref,
    lift_ref, base_ref, coef_ref, coef_in_ref,
    xs_ref, zs_ref, spread_ref, left_ref,
):
    entry, mates = entry_ref[...], partner_ref[...]
    tiles = entry.shape[1] // 128
    elems = faces_ref.shape[1]
    get = spread(mates, spread_ref)
    from_quarter, from_orient = as_int(get(2)), as_int(get(3))
    get = spread(entry, spread_ref)
    to_quarter, to_orient = as_int(get(2)), as_int(get(3))
    for group in range(2 * tiles // 8):
        rows = slice(8 * group, 8 * group + 8)
        swap_in, a_in, b_in = source_matrices(from_quarter[rows], from_orient[rows])
        swap_out, a_out, b_out = target_matrices(to_quarter[rows], to_orient[rows])

        def product(left, right):
            return {
                (r, c): sum(left[r, m] * right[m, c] for m in range(6))
                for r in range(6)
                for c in range(6)
            }

        a, b = product(a_out, a_in), product(b_out, b_in)
        for r in range(6):
            for c in range(6):
                coef_ref[6 * r + c, rows] = jnp.where(swap_out, b[r, c], a[r, c])
                coef_ref[36 + 6 * r + c, rows] = jnp.where(swap_out, a[r, c], b[r, c])
        coef_ref[72, rows] = jnp.where(swap_out != swap_in, 1.0, 0.0)
    get = spread(slot_ref[...], spread_ref)
    swap, a, b = target_matrices(as_int(get(2)), as_int(get(3)))
    put_matrices(coef_in_ref, a, b, swap)
    sums = local_entries(faces_ref, entry, mates, coef_ref, xs_ref, zs_ref, spread_ref, left_ref)
    metric2 = both_lanes(metric_ref[...])
    lift_ref[...] = (LIFTING * metric2) * side_by_side(sums, elems)
    u = u_ref[...]
    base_ref[...] = (DIFFUSION * metric2 * metric2) * mm3(lap_high_ref[...], lap_low_ref[...], u) - both_lanes(pin_ref[...]) * u


def arrived(in_refs, all_ref):
    length = in_refs[0].shape[0]
    for s, ref in enumerate(in_refs):
        all_ref[s * length : (s + 1) * length, :] = ref[...]


def land(y, slot_rows, coef_in_ref, zs_ref, elems, left_ref):
    swap = coef_in_ref[72] > 0.5
    z = swapped(two_axes(y, coef_in_ref, slice(None)), swap)
    zero_pad_rows(zs_ref, 2 * CHANNELS)
    for a in range(6):
        for b in range(6):
            zs_ref[pl.ds(6 * a + b, 2 * CHANNELS, stride=PAD), :] = z[a, b]
    face = jnp.where(slot_rows[4:5] > 0.5, as_int(slot_rows[1:2]), -1)
    sums = scatter_faces(zs_ref, as_int(slot_rows[0:1]), face, elems, left_ref)
    return side_by_side(sums, elems)


def own_share(faces_ref, counts_ref, metric, elems):
    rows = 6 * PAD
    counts, mates = counts_ref[0], counts_ref[1]
    value_w = (0.5 * PENALTY * LIFTING) * metric * (metric * counts + mates)
    deriv_w = (0.5 * LIFTING) * metric * counts

    def faces(kind, comp):
        at = (kind * 2 + comp) * rows
        return faces_ref[at : at + rows, :].astype(F32) + faces_ref[at + 4 * rows : at + 5 * rows, :].astype(F32)

    per_comp = []
    for comp in range(2):
        v, g = faces(0, comp), faces(1, comp)
        blocks = []
        for quarter in range(5):
            for f in range(6):
                at = slice(f * PAD, (f + 1) * PAD)
                row = slice(8 * f + quarter, 8 * f + quarter + 1)
                blocks.append(-(value_w[row] * v[at] + deriv_w[row] * g[at]))
        per_comp.append(jnp.concatenate(blocks, axis=0))
    return jnp.concatenate(per_comp, axis=1)


def finish_first(
    in0, in1, in2, in3, u_ref, faces_ref, slot_ref, metric_ref, counts_ref, coef_ref, coef_in_ref,
    lift_ref, base_ref, own_high_ref, own_low_ref, value_ref, normal_high_ref, normal_low_ref,
    u1_ref, faces1_ref, counts1_ref, msg_ref,
    all_ref, xs_ref, zs_ref, spread_ref, left_ref,
):
    elems = faces_ref.shape[1]
    metric = metric_ref[...]
    slot_rows = slot_ref[...]
    arrived((in0, in1, in2, in3), all_ref)
    stride = 2 * PAD + 8
    own_m = spread(slot_rows, spread_ref)(5)
    mate_m = all_ref[pl.ds(2 * PAD, 8, stride=stride), :]
    y = {}
    for a in range(6):
        for b in range(6):
            n = 6 * a + b
            y[a, b] = (0.5 * PENALTY * own_m) * all_ref[pl.ds(n, 8, stride=stride), :] + all_ref[
                pl.ds(PAD + n, 8, stride=stride), :
            ]
    sums = land(y, slot_rows, coef_in_ref, zs_ref, elems, left_ref)
    lanes = slot_rows.shape[1]
    mate_row = jnp.concatenate(
        [all_ref[s * 2 * stride + 2 * PAD : s * 2 * stride + 2 * PAD + 1, :] for s in range(CHANNELS)], axis=1
    )
    valid = slot_rows[4:5] > 0.5
    kinds = sub_iota((48, lanes)) == as_int(8.0 * slot_rows[1:2] + slot_rows[2:3])
    high, low = split(jnp.where(kinds & valid, mate_row, 0.0))
    hot = one_hot(as_int(slot_rows[0:1]), elems)
    counts1_ref[0] = counts_ref[0]
    counts1_ref[1] = counts_ref[1] + mm_nt(high, hot) + mm_nt(low, hot)
    metric2 = both_lanes(metric)
    lift = lift_ref[...] + (LIFTING * metric2) * sums
    own = own_share(faces_ref, counts1_ref, metric, elems)
    whole = 4 * 6 * PAD
    own = jnp.concatenate([own[:whole], own[whole:] + lift], axis=0)
    node = mm3(own_high_ref[...], own_low_ref[...], own)
    u1 = u_ref[...] + TIME_STEP * (base_ref[...] + DIFFUSION * node)
    u1_ref[...] = u1
    face_tables_of(u1, metric2, value_ref[...], normal_high_ref[...], normal_low_ref[...], faces1_ref)
    send_message(faces1_ref, slot_rows, coef_ref, xs_ref, spread_ref, msg_ref, False, mate_m)


def local_second(
    faces_ref, entry_ref, partner_ref, metric_ref, u0_ref, u_ref, pin_ref, counts_ref, coef_ref,
    lap_high_ref, lap_low_ref, own_high_ref, own_low_ref,
    part_ref,
    xs_ref, zs_ref, spread_ref, left_ref,
):
    elems = faces_ref.shape[1]
    sums = local_entries(
        faces_ref, entry_ref[...], partner_ref[...], coef_ref, xs_ref, zs_ref, spread_ref, left_ref
    )
    metric = metric_ref[...]
    metric2 = both_lanes(metric)
    lift = (LIFTING * metric2) * side_by_side(sums, elems)
    own = own_share(faces_ref, counts_ref, metric, elems)
    whole = 4 * 6 * PAD
    own = jnp.concatenate([own[:whole], own[whole:] + lift], axis=0)
    node = mm3(own_high_ref[...], own_low_ref[...], own)
    u = u_ref[...]
    lap = mm3(lap_high_ref[...], lap_low_ref[...], u)
    rate = DIFFUSION * (metric2 * metric2 * lap + node) - both_lanes(pin_ref[...]) * u
    part_ref[...] = 0.5 * u0_ref[...] + 0.5 * (u + TIME_STEP * rate)


def finish_second(
    in0, in1, in2, in3, part_ref, slot_ref, metric_ref, coef_in_ref, place_ref,
    out_ref,
    all_ref, zs_ref, left_ref,
):
    elems = metric_ref.shape[1]
    arrived((in0, in1, in2, in3), all_ref)
    y = {
        (a, b): all_ref[pl.ds(6 * a + b, 8, stride=PAD), :] for a in range(6) for b in range(6)
    }
    sums = land(y, slot_ref[...], coef_in_ref, zs_ref, elems, left_ref)
    high, low = split((LIFTING * both_lanes(metric_ref[...])) * sums)
    place = place_ref[...]
    node = mm(place, high) + mm(place, low)
    out = part_ref[...] + (0.5 * TIME_STEP * DIFFUSION) * node
    for comp in range(2):
        out_ref[comp] = out[:, comp * elems : (comp + 1) * elems]


def call(kernel, outs, scratch, smem, *args, flops=1e9):
    vmem = pl.BlockSpec(memory_space=pltpu.VMEM)
    scalar = pl.BlockSpec(memory_space=pltpu.SMEM)
    return pl.pallas_call(
        kernel,
        out_shape=[jax.ShapeDtypeStruct(shape, dtype) for shape, dtype in outs],
        in_specs=[scalar] * smem + [vmem] * (len(args) - smem),
        out_specs=[vmem] * len(outs),
        scratch_shapes=[pltpu.VMEM(shape, dtype) for shape, dtype in scratch],
        compiler_params=pltpu.CompilerParams(vmem_limit_bytes=48 * 2**20),
        cost_estimate=pl.CostEstimate(flops=int(flops), bytes_accessed=4000000, transcendentals=0),
    )(*args)


def pairings(count):
    near = [(i, i + 1) for i in range(0, count - 1, 2)]
    across = [(i, i + 1) for i in range(1, count - 1, 2)]
    far = [(i, i + 2) for i in range(count - 2) if i & 2 == 0]
    other = [(i, i + 2) for i in range(count - 2) if i & 2]
    return [[*pairs, *((b, a) for a, b in pairs)] for pairs in (near, across, far, other)]


def exchange(message):
    rows = message.shape[0] // CHANNELS
    routes = pairings(lax.axis_size("slab"))
    return [
        lax.ppermute(message[s * rows : (s + 1) * rows], "slab", routes[s]) for s in range(CHANNELS)
    ]


def on_device(order_field, pinning, metric, elem_count, mortar_table):
    elems = order_field.shape[2]
    lanes = mortar_table.shape[1]
    own_id = lax.axis_index("slab").astype(I32).reshape(1)
    metric_row = metric.reshape(1, elems)
    t = TABLES
    wide = 2 * elems
    rows = 6 * PAD
    slots = CHANNELS * CAP
    both = 2 * lanes // 128
    few = 2 * CHANNELS
    first_rows = few * (2 * PAD + 8)
    second_rows = few * PAD
    u0, faces, entry, mates, slot, counts, coef_out, message = call(
        prepare,
        [
            ((216, wide), F32), ((8 * rows, elems), BF16), ((8, lanes), F32), ((8, lanes), F32),
            ((8, slots), F32), ((2, 48, elems), F32), ((73, few, 128), F32), ((first_rows, 128), F32),
        ],
        [((few * 2 * PAD, 128), F32), ((few * 8, 128), F32)],
        2, own_id, elem_count, order_field, metric_row, mortar_table, t["value"], *t["normal"],
    )
    got = exchange(message)
    lift, base, coef_local, coef_in = call(
        local_first,
        [((rows, wide), F32), ((216, wide), F32), ((73, both, 128), F32), ((73, few, 128), F32)],
        [((both * 2 * PAD, 128), F32), ((both * PAD, 128), F32), ((both * 8, 128), F32), ((4 * rows, lanes), BF16)],
        0, faces, entry, mates, slot, metric_row, u0, pinning, *t["lap"],
    )
    u1, faces1, counts1, message = call(
        finish_first,
        [((216, wide), F32), ((8 * rows, elems), BF16), ((2, 48, elems), F32), ((second_rows, 128), F32)],
        [((first_rows, 128), F32), ((few * 2 * PAD, 128), F32), ((few * PAD, 128), F32), ((few * 8, 128), F32),
         ((4 * rows, slots), BF16)],
        0, *got, u0, faces, slot, metric_row, counts, coef_out, coef_in, lift, base, *t["own"],
        t["value"], *t["normal"],
    )
    got = exchange(message)
    (part,) = call(
        local_second,
        [((216, wide), F32)],
        [((both * 2 * PAD, 128), F32), ((both * PAD, 128), F32), ((both * 8, 128), F32), ((4 * rows, lanes), BF16)],
        0, faces1, entry, mates, metric_row, u0, u1, pinning, counts1, coef_local, *t["lap"], *t["own"],
    )
    (out,) = call(
        finish_second,
        [((2, 216, elems), F32)],
        [((second_rows, 128), F32), ((few * PAD, 128), F32), ((4 * rows, slots), BF16)],
        0, *got, part, slot, metric_row, coef_in, t["place"],
    )
    return out


def solution(mesh):
    split_all = ("groups", "slab")
    return jax.shard_map(
        on_device,
        mesh=mesh,
        in_specs=(
            P(None, None, split_all), P(None, split_all), P(split_all), P(split_all), P(None, split_all),
        ),
        out_specs=P(None, None, split_all),
        check_vma=False,
    )
```

```python
import functools

import jax
import jax.numpy as jnp
import numpy as np
from jax import lax
from jax.experimental import pallas as pl
from jax.experimental.pallas import tpu as pltpu
from jax.sharding import PartitionSpec as P

CAP = 128
CHANNELS = 4
PENALTY = 18.0
LIFTING = 15.0
DIFFUSION = 0.001
TIME_STEP = 0.1
F32 = jnp.float32
BF16 = jnp.bfloat16
I32 = jnp.int32


def gll_points():
    inner_pt = np.sqrt(1.0 / 3.0 - 2.0 * np.sqrt(7.0) / 21.0)
    outer_pt = np.sqrt(1.0 / 3.0 + 2.0 * np.sqrt(7.0) / 21.0)
    return np.array([-1.0, -outer_pt, -inner_pt, inner_pt, outer_pt, 1.0])


def gll_weights(points):
    legendre = (63.0 * points**5 - 70.0 * points**3 + 15.0 * points) / 8.0
    return 2.0 / (30.0 * legendre**2)


def lagrange_matrix(points, targets):
    result = np.ones((targets.shape[0], points.shape[0]))
    for column in range(points.shape[0]):
        for other in range(points.shape[0]):
            if other != column:
                result[:, column] *= (targets - points[other]) / (points[column] - points[other])
    return result


def deriv_matrix(points):
    npoints = points.shape[0]
    factor = np.array(
        [
            np.prod([points[one] - points[other] for other in range(npoints) if other != one])
            for one in range(npoints)
        ]
    )
    result = np.zeros((npoints, npoints))
    for row_no in range(npoints):
        for col_no in range(npoints):
            if row_no != col_no:
                result[row_no, col_no] = factor[row_no] / (
                    factor[col_no] * (points[row_no] - points[col_no])
                )
        result[row_no, row_no] = -np.sum(result[row_no])
    return result


def second_matrix():
    derivative = deriv_matrix(gll_points())
    return np.array(
        [
            [np.sum(derivative[row_no, :] * derivative[:, col_no]) for col_no in range(6)]
            for row_no in range(6)
        ]
    )


def node_at(direction, along_idx, first_idx, second_idx):
    if direction == 0:
        return 36 * along_idx + 6 * first_idx + second_idx
    if direction == 1:
        return 36 * first_idx + 6 * along_idx + second_idx
    return 36 * first_idx + 6 * second_idx + along_idx


FIRST = 76
PAD = 40


def split_np(matrix):
    whole = np.asarray(matrix, np.float32)
    high = whole.astype(BF16)
    return high, (whole - high.astype(np.float32)).astype(BF16)


def constant_tables():
    points = gll_points()
    weights = gll_weights(points)
    derivative = deriv_matrix(points)
    second = second_matrix()
    lap = np.zeros((216, 216))
    for i in range(6):
        for j in range(6):
            for k in range(6):
                row = 36 * i + 6 * j + k
                for m in range(6):
                    lap[row, 36 * m + 6 * j + k] += second[i, m]
                    lap[row, 36 * i + 6 * m + k] += second[j, m]
                    lap[row, 36 * i + 6 * j + m] += second[k, m]
    value = np.zeros((6 * PAD, 216))
    normal = np.zeros((6 * PAD, 216))
    for face in range(6):
        direction, end = face // 2, 5 * (face % 2)
        sign = 1.0 if face % 2 else -1.0
        for a in range(6):
            for b in range(6):
                row = face * PAD + 6 * a + b
                value[row, node_at(direction, end, a, b)] = 1.0
                for m in range(6):
                    normal[row, node_at(direction, m, a, b)] += sign * derivative[end, m]
    to_half = [
        lagrange_matrix(points, (points - 1.0) / 2.0),
        lagrange_matrix(points, (points + 1.0) / 2.0),
    ]
    from_half = [0.5 * half.T * weights[None, :] / weights[:, None] for half in to_half]
    own = [from_half[side] @ to_half[side] for side in range(2)]
    place = value.T
    blocks = []
    for quarter in range(4):
        both = np.zeros((PAD, PAD))
        both[:36, :36] = np.kron(own[quarter // 2], own[quarter % 2])
        blocks.append(place @ np.kron(np.eye(6), both))
    blocks.append(place)
    own_place = np.concatenate(blocks, axis=1)
    return dict(
        traces=np.concatenate([value.astype(BF16), *split_np(normal)], axis=0),
        rate=np.concatenate(split_np(np.concatenate([own_place, lap], axis=1)), axis=0),
        place=place.astype(BF16),
        to_half=to_half,
        from_half=from_half,
    )


TABLES = constant_tables()


def split(x):
    high = x.astype(BF16)
    return high, (x - high.astype(F32)).astype(BF16)


def mm(a, b):
    return jnp.dot(a, b, preferred_element_type=F32)


def mm_nt(a, b):
    return lax.dot_general(a, b, (((1,), (1,)), ((), ())), preferred_element_type=F32)


def mm3(const_high, const_low, x):
    high, low = split(x)
    return mm(const_high, high) + mm(const_high, low) + mm(const_low, high)


def sub_iota(shape):
    return lax.broadcasted_iota(I32, shape, 0)


def one_hot(row, length):
    return jnp.where(sub_iota((length, row.shape[1])) == row, 1.0, 0.0).astype(BF16)


def as_int(row):
    return row.astype(I32)


def stack_rows(rows, lanes):
    at = sub_iota((8, lanes))
    out = jnp.zeros((8, lanes), F32)
    for place, row in enumerate(rows):
        out = jnp.where(at == place, row, out)
    return out


def face_tables_of(u, metric2, traces, table_ref):
    elems = u.shape[1] // 2
    high, low = split(u)
    third = 6 * PAD
    value, normal_high, normal_low = (traces[n * third : (n + 1) * third] for n in range(3))
    v_parts = (mm(value, high).astype(BF16), mm(value, low).astype(BF16))
    g = (mm(normal_high, high) + mm(normal_high, low) + mm(normal_low, high)) * metric2
    g_parts = split(g)
    rows = 6 * PAD
    for part in range(2):
        for kind, parts in enumerate((v_parts, g_parts)):
            for comp in range(2):
                at = ((part * 2 + kind) * 2 + comp) * rows
                table_ref[at : at + rows, :] = parts[part][:, comp * elems : (comp + 1) * elems]


def gather_faces(table_ref, elem_row, face_row, out_ref):
    elems = table_ref.shape[1]
    rows = 6 * PAD
    lanes = elem_row.shape[1]
    step = 256
    for start in range(0, lanes, step):
        hot = one_hot(elem_row[:, start : start + step], elems)
        got = mm(table_ref[...], hot)
        face = face_row[:, start : start + step]
        for kind in range(2):
            for comp in range(2):
                at = (kind * 2 + comp) * rows
                low_at = at + 4 * rows
                picked = got[at : at + PAD] + got[low_at : low_at + PAD]
                for f in range(1, 6):
                    mine = (
                        got[at + f * PAD : at + (f + 1) * PAD]
                        + got[low_at + f * PAD : low_at + (f + 1) * PAD]
                    )
                    picked = jnp.where(face == f, mine, picked)
                for t in range(step // 128):
                    tile = start // 128 + t
                    to = (2 * tile + comp) * 2 * PAD + kind * PAD
                    out_ref[to : to + PAD, :] = picked[:, t * 128 : (t + 1) * 128]


def spread(att, ref):
    tiles = att.shape[1] // 128
    for tile in range(tiles):
        for comp in range(2):
            at = (2 * tile + comp) * 8
            ref[at : at + 8, :] = att[:, tile * 128 : (tile + 1) * 128]

    def get(row):
        return ref[pl.ds(row, 2 * tiles, stride=8), :]

    return get


def axis_classes(quarter, orient):
    swap = (orient & 4) > 0
    first = quarter // 2
    second = quarter - 2 * first
    whole = quarter == 4
    a = jnp.where(whole, 2, jnp.where(swap, second, first))
    b = jnp.where(whole, 2, jnp.where(swap, first, second))
    return swap, a, b, (orient & 1) > 0, (orient & 2) > 0


def axis_matrix(cls, flip, halves, flip_rows):
    out = {}
    is0, is1 = cls == 0, cls == 1
    for r in range(6):
        for c in range(6):

            def entry(r0, c0):
                return jnp.where(
                    is0,
                    float(halves[0][r0, c0]),
                    jnp.where(is1, float(halves[1][r0, c0]), 1.0 if r0 == c0 else 0.0),
                )

            flipped = entry(5 - r, c) if flip_rows else entry(r, 5 - c)
            out[r, c] = jnp.where(flip, flipped, entry(r, c))
    return out


def source_matrices(quarter, orient):
    swap, a, b, flip_a, flip_b = axis_classes(quarter, orient)
    halves = TABLES["to_half"]
    return swap, axis_matrix(a, flip_a, halves, True), axis_matrix(b, flip_b, halves, True)


def target_matrices(quarter, orient):
    swap, a, b, flip_a, flip_b = axis_classes(quarter, orient)
    halves = TABLES["from_half"]
    return swap, axis_matrix(a, flip_a, halves, False), axis_matrix(b, flip_b, halves, False)


def put_matrices(ref, a, b, swap):
    for r in range(6):
        for c in range(6):
            ref[6 * r + c] = a[r, c]
            ref[36 + 6 * r + c] = b[r, c]
    ref[72] = jnp.where(swap, 1.0, 0.0)


def two_axes(x, coef, rows):
    y = {}
    for b in range(6):
        for r in range(6):
            acc = coef[6 * r, rows] * x[0, b]
            for a in range(1, 6):
                acc = acc + coef[6 * r + a, rows] * x[a, b]
            y[r, b] = acc
    z = {}
    for r in range(6):
        for s in range(6):
            acc = coef[36 + 6 * s, rows] * y[r, 0]
            for b in range(1, 6):
                acc = acc + coef[36 + 6 * s + b, rows] * y[r, b]
            z[r, s] = acc
    return z


def swapped(x, swap):
    return {
        (a, b): x[a, b] if a == b else jnp.where(swap, x[b, a], x[a, b])
        for a in range(6)
        for b in range(6)
    }


def scatter_faces(z_ref, elem_row, face_row, elems, left_ref):
    lanes = elem_row.shape[1]
    width = 6 * 2 * PAD
    for tile in range(lanes // 128):
        at = slice(tile * 128, (tile + 1) * 128)
        high, low = split(z_ref[tile * 2 * PAD : (tile + 1) * 2 * PAD, :])
        face = face_row[:, at]
        for f in range(6):
            mask = jnp.where(face == f, 1.0, 0.0).astype(BF16)
            left_ref[f * 2 * PAD : (f + 1) * 2 * PAD, at] = high * mask
            left_ref[width + f * 2 * PAD : width + (f + 1) * 2 * PAD, at] = low * mask
    hot = one_hot(elem_row, elems)
    both = mm_nt(left_ref[...], hot)
    return both[:width] + both[width:]


def side_by_side(sums, elems):
    out = []
    for f in range(6):
        at = f * 2 * PAD
        out.append(jnp.concatenate([sums[at : at + PAD], sums[at + PAD : at + 2 * PAD]], axis=1))
    return jnp.concatenate(out, axis=0)


def zero_pad_rows(ref, blocks):
    for block in range(blocks):
        ref[block * PAD + 32 : block * PAD + 40, :] = jnp.zeros((8, 128), F32)


def both_lanes(x):
    return jnp.concatenate([x, x], axis=1)


def send_message(table_ref, slot_rows, coef_ref, xs_ref, spread_ref, out_ref, sent, first, mp=None):
    gather_faces(table_ref, as_int(slot_rows[0:1]), as_int(slot_rows[1:2]), xs_ref)
    get = spread(slot_rows, spread_ref)
    own_m = get(5)
    rows = slice(None)
    swap = coef_ref[72] > 0.5

    def load(kind):
        return {
            (a, b): xs_ref[pl.ds(kind * PAD + 6 * a + b, 2 * CHANNELS, stride=2 * PAD), :]
            for a in range(6)
            for b in range(6)
        }

    if first:
        v = two_axes(swapped(load(0), swap), coef_ref, rows)
        g = two_axes(swapped(load(1), swap), coef_ref, rows)
        for a in range(6):
            for b in range(6):
                n = 6 * a + b
                out_ref[pl.ds(n, 8, stride=FIRST), :] = v[a, b]
                out_ref[pl.ds(36 + n, 8, stride=FIRST), :] = (0.5 * PENALTY * own_m) * v[a, b] - 0.5 * g[a, b]
        for n in range(72, FIRST):
            out_ref[pl.ds(n, 8, stride=FIRST), :] = own_m
    else:
        tau = 0.5 * PENALTY * (own_m + mp)
        v, g = load(0), load(1)
        x = {key: tau * v[key] - 0.5 * g[key] for key in v}
        z = two_axes(swapped(x, swap), coef_ref, rows)
        for a in range(6):
            for b in range(6):
                out_ref[pl.ds(6 * a + b, 8, stride=36), :] = z[a, b]
    rows = out_ref.shape[0] // CHANNELS
    near_ref, far_ref, other_ref = sent
    near_ref[...] = out_ref[0:rows, :]
    for place, ref in enumerate((far_ref, other_ref)):
        ref[0:rows, :] = out_ref[(2 + place) * rows : (3 + place) * rows, :]
        ref[rows : 2 * rows, :] = out_ref[rows : 2 * rows, :]


def prepare(
    own_ref, count_ref, table_hbm, metric_hbm, field_hbm, traces_hbm,
    metric_ref, u_ref, faces_ref, entry_ref, partner_ref, slot_ref, counts_ref, coef_ref, near_ref, far_ref, other_ref,
    msg_ref, table_ref, field_ref, traces_ref, xs_ref, spread_ref, sems,
):
    pairs = (
        (table_hbm, table_ref), (metric_hbm, metric_ref), (field_hbm, field_ref), (traces_hbm, traces_ref),
    )
    copies = [
        pltpu.make_async_copy(source, target, sems.at[place])
        for place, (source, target) in enumerate(pairs)
    ]
    for copy in copies:
        copy.start()
    for copy in copies[:2]:
        copy.wait()
    elems = field_ref.shape[2]
    lanes = table_ref.shape[1]
    tiles = lanes // 128
    own = own_ref[0]
    metric = metric_ref[...]
    element, face, quarter, orient, partner, link = (table_ref[r : r + 1, :] for r in range(6))
    used = partner >= 0
    local = partner == own
    distance = partner - own
    near = 1 - 2 * (own & 1)
    far = 2 - 2 * (own & 2)
    channel = jnp.where(
        distance == near, 0, jnp.where(distance == -near, 1, jnp.where(distance == far, 2, 3))
    )
    channel = jnp.where(used & jnp.logical_not(local), channel, -1)
    m1 = metric.astype(BF16).astype(F32)
    m2 = (metric - m1).astype(BF16).astype(F32)
    m3 = metric - m1 - m2
    hot = one_hot(element, elems)
    metric_rows = mm(stack_rows([m1, m2, m3], elems).astype(BF16), hot)
    parts = [metric_rows[r : r + 1] for r in range(3)]
    att = stack_rows([element.astype(F32), face.astype(F32), quarter.astype(F32), orient.astype(F32),
                      jnp.where(used, 1.0, 0.0)] + parts, lanes)
    link_hot = one_hot(link & (CAP - 1), CAP)
    left = jnp.concatenate([jnp.where(channel == s, att, 0.0) for s in range(CHANNELS)], axis=0)
    slots = mm_nt(left.astype(BF16), link_hot)
    slots = jnp.concatenate([slots[8 * s : 8 * s + 8] for s in range(CHANNELS)], axis=1)

    def finished(rows8, n):
        total = rows8[5:6] + rows8[6:7] + rows8[7:8]
        return jnp.where(sub_iota((8, n)) == 5, total, rows8)

    slot_rows = finished(slots, CHANNELS * CAP)
    slot_ref[...] = slot_rows
    left = jnp.concatenate([att[:, t * 128 : (t + 1) * 128] for t in range(tiles)], axis=0)
    spots = mm(left.astype(BF16), link_hot)
    high_link = link // CAP
    mates = spots[0:8]
    for t in range(1, tiles):
        mates = jnp.where(high_link == t, spots[8 * t : 8 * t + 8], mates)
    mates = finished(mates, lanes)
    partner_ref[...] = mates
    entry = finished(att, lanes)
    entry = jnp.where((sub_iota((8, lanes)) == 4) & jnp.logical_not(local), 0.0, entry)
    entry_ref[...] = entry
    kinds = sub_iota((48, lanes)) == 8 * face + quarter
    counts_ref[0] = mm_nt(jnp.where(kinds & used, 1.0, 0.0).astype(BF16), hot)
    weight = jnp.where(kinds & local, mates[5:6], 0.0)
    high, low = split(weight)
    counts_ref[1] = mm_nt(high, hot) + mm_nt(low, hot)

    get = spread(slot_rows, spread_ref)
    swap, a, b = source_matrices(as_int(get(2)), as_int(get(3)))
    put_matrices(coef_ref, a, b, swap)
    for copy in copies[2:]:
        copy.wait()
    alive = lax.broadcasted_iota(I32, (1, elems), 1) < count_ref[0]
    u = jnp.concatenate([jnp.where(alive, field_ref[comp], 0.0) for comp in range(2)], axis=1)
    u_ref[...] = u
    face_tables_of(
        u, both_lanes(metric), traces_ref[...], faces_ref
    )
    sent = (near_ref, far_ref, other_ref)
    send_message(faces_ref, slot_rows, coef_ref, xs_ref, spread_ref, msg_ref, sent, True)


def local_entries(faces_ref, entry, mates, coef_ref, xs_ref, zs_ref, spread_ref, left_ref):
    lanes = entry.shape[1]
    tiles = lanes // 128
    elems = faces_ref.shape[1]
    gather_faces(faces_ref, as_int(mates[0:1]), as_int(mates[1:2]), xs_ref)
    own_m = spread(entry, spread_ref)(5)
    mate_m = spread(mates, spread_ref)(5)
    tau_all = 0.5 * PENALTY * (own_m + mate_m)
    zero_pad_rows(zs_ref, 2 * tiles)
    for group in range(2 * tiles // 8):
        rows = slice(8 * group, 8 * group + 8)
        base = 8 * group * 2 * PAD
        tau = tau_all[rows]
        swap = coef_ref[72, rows] > 0.5
        x = {}
        for a in range(6):
            for b in range(6):
                n = 6 * a + b
                v = xs_ref[pl.ds(base + n, 8, stride=2 * PAD), :]
                g = xs_ref[pl.ds(base + PAD + n, 8, stride=2 * PAD), :]
                x[a, b] = tau * v - 0.5 * g
        z = two_axes(swapped(x, swap), coef_ref, rows)
        for a in range(6):
            for b in range(6):
                zs_ref[pl.ds(8 * group * PAD + 6 * a + b, 8, stride=PAD), :] = z[a, b]
    face = jnp.where(entry[4:5] > 0.5, as_int(entry[1:2]), -1)
    return scatter_faces(zs_ref, as_int(entry[0:1]), face, elems, left_ref)


def local_first(
    near_ref, faces_ref, entry_ref, partner_ref, slot_ref, metric_ref, u_ref, pin_ref, counts_ref,
    rate_ref,
    near_out_ref, part_ref, coef_ref, coef_in_ref,
    xs_ref, zs_ref, spread_ref, left_ref,
):
    near_out_ref[...] = near_ref[...]
    entry, mates = entry_ref[...], partner_ref[...]
    tiles = entry.shape[1] // 128
    elems = faces_ref.shape[1]
    get = spread(mates, spread_ref)
    from_quarter, from_orient = as_int(get(2)), as_int(get(3))
    get = spread(entry, spread_ref)
    to_quarter, to_orient = as_int(get(2)), as_int(get(3))
    for group in range(2 * tiles // 8):
        rows = slice(8 * group, 8 * group + 8)
        swap_in, a_in, b_in = source_matrices(from_quarter[rows], from_orient[rows])
        swap_out, a_out, b_out = target_matrices(to_quarter[rows], to_orient[rows])

        def product(left, right):
            return {
                (r, c): sum(left[r, m] * right[m, c] for m in range(6))
                for r in range(6)
                for c in range(6)
            }

        a, b = product(a_out, a_in), product(b_out, b_in)
        for r in range(6):
            for c in range(6):
                coef_ref[6 * r + c, rows] = jnp.where(swap_out, b[r, c], a[r, c])
                coef_ref[36 + 6 * r + c, rows] = jnp.where(swap_out, a[r, c], b[r, c])
        coef_ref[72, rows] = jnp.where(swap_out != swap_in, 1.0, 0.0)
    get = spread(slot_ref[...], spread_ref)
    swap, a, b = target_matrices(as_int(get(2)), as_int(get(3)))
    put_matrices(coef_in_ref, a, b, swap)
    sums = local_entries(faces_ref, entry, mates, coef_ref, xs_ref, zs_ref, spread_ref, left_ref)
    rate = known_rate(
        sums, faces_ref, counts_ref[0], counts_ref[1], metric_ref[...], u_ref[...], pin_ref[...],
        rate_ref,
    )
    part_ref[...] = u_ref[...] + TIME_STEP * rate


def arrived(swap_ref, far_ref, other_ref, all_ref):
    rows = swap_ref.shape[0] // 2
    all_ref[0 : 2 * rows, :] = swap_ref[...]
    all_ref[2 * rows : 3 * rows, :] = far_ref[0:rows, :]
    all_ref[3 * rows : 4 * rows, :] = other_ref[0:rows, :]


def land(y, slot_rows, coef_in_ref, zs_ref, elems, left_ref):
    swap = coef_in_ref[72] > 0.5
    z = swapped(two_axes(y, coef_in_ref, slice(None)), swap)
    zero_pad_rows(zs_ref, 2 * CHANNELS)
    for a in range(6):
        for b in range(6):
            zs_ref[pl.ds(6 * a + b, 2 * CHANNELS, stride=PAD), :] = z[a, b]
    face = jnp.where(slot_rows[4:5] > 0.5, as_int(slot_rows[1:2]), -1)
    sums = scatter_faces(zs_ref, as_int(slot_rows[0:1]), face, elems, left_ref)
    return side_by_side(sums, elems)


def known_rate(
    sums, faces_ref, counts, mates, metric, u, pin, rate_ref,
):
    elems = faces_ref.shape[1]
    metric2 = both_lanes(metric)
    lift = (LIFTING * metric2) * side_by_side(sums, elems)
    own = own_share(faces_ref, counts, mates, metric, elems)
    whole = 4 * 6 * PAD
    terms = jnp.concatenate([own[:whole], own[whole:] + lift, (metric2 * metric2) * u], axis=0)
    nodes = u.shape[0]
    high, low = split(terms)
    both = mm(rate_ref[...], high)
    return DIFFUSION * (both[:nodes] + both[nodes:] + mm(rate_ref[0:nodes, :], low)) - both_lanes(pin) * u


def own_share(faces_ref, counts, mates, metric, elems):
    rows = 6 * PAD
    value_w = (0.5 * PENALTY * LIFTING) * metric * (metric * counts + mates)
    deriv_w = (0.5 * LIFTING) * metric * counts

    def faces(kind, comp):
        at = (kind * 2 + comp) * rows
        return faces_ref[at : at + rows, :].astype(F32) + faces_ref[at + 4 * rows : at + 5 * rows, :].astype(F32)

    per_comp = []
    for comp in range(2):
        v, g = faces(0, comp), faces(1, comp)
        blocks = []
        for quarter in range(5):
            for f in range(6):
                at = slice(f * PAD, (f + 1) * PAD)
                row = slice(8 * f + quarter, 8 * f + quarter + 1)
                blocks.append(-(value_w[row] * v[at] + deriv_w[row] * g[at]))
        per_comp.append(jnp.concatenate(blocks, axis=0))
    return jnp.concatenate(per_comp, axis=1)


def placed(sums, metric, place_ref):
    high, low = split((LIFTING * both_lanes(metric)) * sums)
    place = place_ref[...]
    return mm(place, high) + mm(place, low)


def finish_first(
    in_swap, in_other, in_far, near_sent, far_sent, other_sent, part_ref, slot_ref, metric_ref, coef_ref, coef_in_ref,
    place_ref, traces_ref,
    u1_ref, faces1_ref, mate_ref, near_ref, far_ref, other_ref,
    msg_ref, all_ref, own_ref, xs_ref, zs_ref, spread_ref, left_ref,
):
    elems = faces1_ref.shape[1]
    metric = metric_ref[...]
    slot_rows = slot_ref[...]
    arrived(in_swap, in_far, in_other, all_ref)
    block = near_sent.shape[0]
    own_ref[0:block, :] = near_sent[...]
    own_ref[block : 2 * block, :] = far_sent[block : 2 * block, :]
    own_ref[2 * block : 3 * block, :] = far_sent[0:block, :]
    own_ref[3 * block : 4 * block, :] = other_sent[0:block, :]
    own_m = spread(slot_rows, spread_ref)(5)
    mate_m = all_ref[pl.ds(72, 8, stride=FIRST), :]
    y = {}
    for a in range(6):
        for b in range(6):
            n = 6 * a + b
            theirs, ours = all_ref[pl.ds(n, 8, stride=FIRST), :], own_ref[pl.ds(n, 8, stride=FIRST), :]
            y[a, b] = (0.5 * PENALTY) * (own_m * theirs - mate_m * ours) + all_ref[pl.ds(36 + n, 8, stride=FIRST), :]
    sums = land(y, slot_rows, coef_in_ref, zs_ref, elems, left_ref)
    mate_ref[...] = jnp.concatenate(
        [all_ref[s * block + 72 : s * block + 73, :] for s in range(CHANNELS)], axis=1
    )
    u1 = part_ref[...] + (TIME_STEP * DIFFUSION) * placed(sums, metric, place_ref)
    u1_ref[...] = u1
    face_tables_of(u1, both_lanes(metric), traces_ref[...], faces1_ref)
    sent = (near_ref, far_ref, other_ref)
    send_message(faces1_ref, slot_rows, coef_ref, xs_ref, spread_ref, msg_ref, sent, False, mate_m)


def local_second(
    near_ref, faces_ref, entry_ref, partner_ref, slot_ref, mate_ref, metric_ref, u0_ref, u_ref, pin_ref, counts_ref,
    coef_ref, rate_ref,
    near_out_ref, part_ref,
    xs_ref, zs_ref, spread_ref, left_ref,
):
    near_out_ref[...] = near_ref[...]
    elems = faces_ref.shape[1]
    sums = local_entries(
        faces_ref, entry_ref[...], partner_ref[...], coef_ref, xs_ref, zs_ref, spread_ref, left_ref
    )
    slot_rows = slot_ref[...]
    kinds = sub_iota((48, slot_rows.shape[1])) == as_int(8.0 * slot_rows[1:2] + slot_rows[2:3])
    high, low = split(jnp.where(kinds & (slot_rows[4:5] > 0.5), mate_ref[...], 0.0))
    hot = one_hot(as_int(slot_rows[0:1]), elems)
    mates = counts_ref[1] + mm_nt(high, hot) + mm_nt(low, hot)
    u = u_ref[...]
    rate = known_rate(
        sums, faces_ref, counts_ref[0], mates, metric_ref[...], u, pin_ref[...],
        rate_ref,
    )
    part_ref[...] = 0.5 * u0_ref[...] + 0.5 * (u + TIME_STEP * rate)


def finish_second(
    in_swap, in_other, in_far, part_ref, slot_ref, metric_ref, coef_in_ref, place_ref,
    out_ref,
    all_ref, zs_ref, left_ref,
):
    elems = metric_ref.shape[1]
    arrived(in_swap, in_far, in_other, all_ref)
    y = {(a, b): all_ref[pl.ds(6 * a + b, 8, stride=36), :] for a in range(6) for b in range(6)}
    sums = land(y, slot_ref[...], coef_in_ref, zs_ref, elems, left_ref)
    out = part_ref[...] + (0.5 * TIME_STEP * DIFFUSION) * placed(sums, metric_ref[...], place_ref)
    for comp in range(2):
        out_ref[comp] = out[:, comp * elems : (comp + 1) * elems]


def call(kernel, outs, scratch, *args, smem=0, copies=0):
    vmem = pl.BlockSpec(memory_space=pltpu.VMEM)
    scalar = pl.BlockSpec(memory_space=pltpu.SMEM)
    given = pl.BlockSpec(memory_space=pl.ANY) if copies else vmem
    scratch_shapes = [pltpu.VMEM(shape, dtype) for shape, dtype in scratch]
    if copies:
        scratch_shapes.append(pltpu.SemaphoreType.DMA((copies,)))
    return pl.pallas_call(
        kernel,
        out_shape=[jax.ShapeDtypeStruct(shape, dtype) for shape, dtype in outs],
        in_specs=[scalar] * smem + [given] * (len(args) - smem),
        out_specs=[vmem] * len(outs),
        scratch_shapes=scratch_shapes,
        compiler_params=pltpu.CompilerParams(vmem_limit_bytes=(53 if copies else 16) * 2**20),
        cost_estimate=pl.CostEstimate(flops=10**9, bytes_accessed=4000000, transcendentals=0),
    )(*args)


def pairings(count):
    near = [(i, i + 1) for i in range(0, count - 1, 2)]
    far = [(i, i + 2) for i in range(count - 2) if i & 2 == 0]
    other = [(i, i + 2) for i in range(count - 2) if i & 2]
    return [[*pairs, *((b, a) for a, b in pairs)] for pairs in (near, far, other)]


def cross_exchange(far, other):
    _, far_route, other_route = pairings(lax.axis_size("slab"))
    other = lax.ppermute(other, "slab", other_route)
    far = lax.ppermute(far, "slab", far_route)
    return far, other


def sibling_exchange(near, far, other):
    own = lax.axis_index("slab")
    rows = near.shape[0]
    from_other = ((own ^ (own >> 1)) & 1) == 1
    relayed = jnp.where(from_other, other[rows:], far[rows:])
    near_route = pairings(lax.axis_size("slab"))[0]
    return lax.ppermute(jnp.concatenate([near, relayed], axis=0), "slab", near_route)


def on_device(order_field, pinning, metric, elem_count, mortar_table):
    elems = order_field.shape[2]
    lanes = mortar_table.shape[1]
    own_id = lax.axis_index("slab").astype(I32).reshape(1)
    wide = 2 * elems
    rows = 6 * PAD
    slots = CHANNELS * CAP
    both = 2 * lanes // 128
    few = 2 * CHANNELS
    first_rows = few * FIRST
    second_rows = few * 36
    first_sent = [((n * first_rows // CHANNELS, 128), F32) for n in (1, 2, 2)]
    second_sent = [((n * second_rows // CHANNELS, 128), F32) for n in (1, 2, 2)]
    field_out = ((216, wide), F32)
    faces_out = ((8 * rows, elems), BF16)
    few_scratch = [((few * 2 * PAD, 128), F32), ((few * PAD, 128), F32), ((few * 8, 128), F32), ((4 * rows, slots), BF16)]
    both_scratch = [((both * 2 * PAD, 128), F32), ((both * PAD, 128), F32), ((both * 8, 128), F32), ((4 * rows, lanes), BF16)]
    traces, rate, place = (TABLES[name] for name in ("traces", "rate", "place"))
    metric_row, u0, faces, entry, mates, slot, counts, coef_out, near, far, other = call(
        prepare,
        [
            ((1, elems), F32), field_out, faces_out, ((8, lanes), F32), ((8, lanes), F32),
            ((8, slots), F32), ((2, 48, elems), F32), ((73, few, 128), F32), *first_sent,
        ],
        [
            ((first_rows, 128), F32), (mortar_table.shape, I32), (order_field.shape, F32), (traces.shape, BF16),
            few_scratch[0], few_scratch[2],
        ],
        own_id, elem_count, mortar_table, metric.reshape(1, elems), order_field, traces,
        smem=2, copies=4,
    )
    got_far, got_other = cross_exchange(far, other)
    passed, part, coef_local, coef_in = call(
        local_first,
        [first_sent[0], field_out, ((73, both, 128), F32), ((73, few, 128), F32)],
        both_scratch,
        near, faces, entry, mates, slot, metric_row, u0, pinning, counts, rate,
    )
    got_swap = sibling_exchange(passed, got_far, got_other)
    u1, faces1, mate_row, near, far, other = call(
        finish_first,
        [field_out, faces_out, ((1, slots), F32), *second_sent],
        [((second_rows, 128), F32), ((first_rows, 128), F32), ((first_rows, 128), F32), *few_scratch],
        got_swap, got_other, got_far, near, far, other, part, slot, metric_row, coef_out, coef_in,
        place, traces,
    )
    got_far, got_other = cross_exchange(far, other)
    passed, part = call(
        local_second,
        [second_sent[0], field_out],
        both_scratch,
        near, faces1, entry, mates, slot, mate_row, metric_row, u0, u1, pinning, counts, coef_local,
        rate,
    )
    got_swap = sibling_exchange(passed, got_far, got_other)
    (out,) = call(
        finish_second,
        [(order_field.shape, F32)],
        [((second_rows, 128), F32), few_scratch[1], few_scratch[3]],
        got_swap, got_other, got_far, part, slot, metric_row, coef_in, place,
    )
    return out


def solution(mesh):
    split_all = ("groups", "slab")
    return jax.shard_map(
        on_device,
        mesh=mesh,
        in_specs=(
            P(None, None, split_all), P(None, split_all), P(split_all), P(split_all), P(None, split_all),
        ),
        out_specs=P(None, None, split_all),
        check_vma=False,
    )
```

```python
import functools

import jax
import jax.numpy as jnp
import numpy as np
from jax import lax
from jax.experimental import pallas as pl
from jax.experimental.pallas import tpu as pltpu
from jax.sharding import PartitionSpec as P

CAP = 128
CHANNELS = 4
PENALTY = 18.0
LIFTING = 15.0
DIFFUSION = 0.001
TIME_STEP = 0.1
F32 = jnp.float32
BF16 = jnp.bfloat16
I32 = jnp.int32


def gll_points():
    inner_pt = np.sqrt(1.0 / 3.0 - 2.0 * np.sqrt(7.0) / 21.0)
    outer_pt = np.sqrt(1.0 / 3.0 + 2.0 * np.sqrt(7.0) / 21.0)
    return np.array([-1.0, -outer_pt, -inner_pt, inner_pt, outer_pt, 1.0])


def gll_weights(points):
    legendre = (63.0 * points**5 - 70.0 * points**3 + 15.0 * points) / 8.0
    return 2.0 / (30.0 * legendre**2)


def lagrange_matrix(points, targets):
    result = np.ones((targets.shape[0], points.shape[0]))
    for column in range(points.shape[0]):
        for other in range(points.shape[0]):
            if other != column:
                result[:, column] *= (targets - points[other]) / (points[column] - points[other])
    return result


def deriv_matrix(points):
    npoints = points.shape[0]
    factor = np.array(
        [
            np.prod([points[one] - points[other] for other in range(npoints) if other != one])
            for one in range(npoints)
        ]
    )
    result = np.zeros((npoints, npoints))
    for row_no in range(npoints):
        for col_no in range(npoints):
            if row_no != col_no:
                result[row_no, col_no] = factor[row_no] / (
                    factor[col_no] * (points[row_no] - points[col_no])
                )
        result[row_no, row_no] = -np.sum(result[row_no])
    return result


def second_matrix():
    derivative = deriv_matrix(gll_points())
    return np.array(
        [
            [np.sum(derivative[row_no, :] * derivative[:, col_no]) for col_no in range(6)]
            for row_no in range(6)
        ]
    )


def node_at(direction, along_idx, first_idx, second_idx):
    if direction == 0:
        return 36 * along_idx + 6 * first_idx + second_idx
    if direction == 1:
        return 36 * first_idx + 6 * along_idx + second_idx
    return 36 * first_idx + 6 * second_idx + along_idx


FIRST = 76
PAD = 40


def split_np(matrix):
    whole = np.asarray(matrix, np.float32)
    high = whole.astype(BF16)
    return high, (whole - high.astype(np.float32)).astype(BF16)


def constant_tables():
    points = gll_points()
    weights = gll_weights(points)
    derivative = deriv_matrix(points)
    second = second_matrix()
    lap = np.zeros((216, 216))
    for i in range(6):
        for j in range(6):
            for k in range(6):
                row = 36 * i + 6 * j + k
                for m in range(6):
                    lap[row, 36 * m + 6 * j + k] += second[i, m]
                    lap[row, 36 * i + 6 * m + k] += second[j, m]
                    lap[row, 36 * i + 6 * j + m] += second[k, m]
    value = np.zeros((6 * PAD, 216))
    normal = np.zeros((6 * PAD, 216))
    for face in range(6):
        direction, end = face // 2, 5 * (face % 2)
        sign = 1.0 if face % 2 else -1.0
        for a in range(6):
            for b in range(6):
                row = face * PAD + 6 * a + b
                value[row, node_at(direction, end, a, b)] = 1.0
                for m in range(6):
                    normal[row, node_at(direction, m, a, b)] += sign * derivative[end, m]
    to_half = [
        lagrange_matrix(points, (points - 1.0) / 2.0),
        lagrange_matrix(points, (points + 1.0) / 2.0),
    ]
    from_half = [0.5 * half.T * weights[None, :] / weights[:, None] for half in to_half]
    own = [from_half[side] @ to_half[side] for side in range(2)]
    place = value.T
    blocks = []
    for quarter in range(4):
        both = np.zeros((PAD, PAD))
        both[:36, :36] = np.kron(own[quarter // 2], own[quarter % 2])
        blocks.append(place @ np.kron(np.eye(6), both))
    blocks.append(place)
    own_place = np.concatenate(blocks, axis=1)
    return dict(
        traces=np.concatenate([value.astype(BF16), *split_np(normal)], axis=0),
        rate=np.concatenate(split_np(np.concatenate([own_place, lap], axis=1)), axis=0),
        place=place.astype(BF16),
        to_half=to_half,
        from_half=from_half,
    )


TABLES = constant_tables()


def split(x):
    high = x.astype(BF16)
    return high, (x - high.astype(F32)).astype(BF16)


def mm(a, b):
    return jnp.dot(a, b, preferred_element_type=F32)


def mm_nt(a, b):
    return lax.dot_general(a, b, (((1,), (1,)), ((), ())), preferred_element_type=F32)


def mm3(const_high, const_low, x):
    high, low = split(x)
    return mm(const_high, high) + mm(const_high, low) + mm(const_low, high)


def sub_iota(shape):
    return lax.broadcasted_iota(I32, shape, 0)


def one_hot(row, length):
    return jnp.where(sub_iota((length, row.shape[1])) == row, 1.0, 0.0).astype(BF16)


def as_int(row):
    return row.astype(I32)


def stack_rows(rows, lanes):
    at = sub_iota((8, lanes))
    out = jnp.zeros((8, lanes), F32)
    for place, row in enumerate(rows):
        out = jnp.where(at == place, row, out)
    return out


def face_tables_of(u, metric2, traces, table_ref):
    elems = u.shape[1] // 2
    high, low = split(u)
    third = 6 * PAD
    value, normal_high, normal_low = (traces[n * third : (n + 1) * third] for n in range(3))
    v_parts = (mm(value, high).astype(BF16), mm(value, low).astype(BF16))
    g = (mm(normal_high, high) + mm(normal_high, low) + mm(normal_low, high)) * metric2
    g_parts = split(g)
    rows = 6 * PAD
    for part in range(2):
        for kind, parts in enumerate((v_parts, g_parts)):
            for comp in range(2):
                at = ((part * 2 + kind) * 2 + comp) * rows
                table_ref[at : at + rows, :] = parts[part][:, comp * elems : (comp + 1) * elems]


def gather_faces(table_ref, elem_row, face_row, out_ref):
    elems = table_ref.shape[1]
    rows = 6 * PAD
    lanes = elem_row.shape[1]
    step = 256
    for start in range(0, lanes, step):
        hot = one_hot(elem_row[:, start : start + step], elems)
        got = mm(table_ref[...], hot)
        face = face_row[:, start : start + step]
        for kind in range(2):
            for comp in range(2):
                at = (kind * 2 + comp) * rows
                low_at = at + 4 * rows
                picked = got[at : at + PAD] + got[low_at : low_at + PAD]
                for f in range(1, 6):
                    mine = (
                        got[at + f * PAD : at + (f + 1) * PAD]
                        + got[low_at + f * PAD : low_at + (f + 1) * PAD]
                    )
                    picked = jnp.where(face == f, mine, picked)
                for t in range(step // 128):
                    tile = start // 128 + t
                    to = (2 * tile + comp) * 2 * PAD + kind * PAD
                    out_ref[to : to + PAD, :] = picked[:, t * 128 : (t + 1) * 128]


def spread(att, ref):
    tiles = att.shape[1] // 128
    for tile in range(tiles):
        for comp in range(2):
            at = (2 * tile + comp) * 8
            ref[at : at + 8, :] = att[:, tile * 128 : (tile + 1) * 128]

    def get(row):
        return ref[pl.ds(row, 2 * tiles, stride=8), :]

    return get


def axis_classes(quarter, orient):
    swap = (orient & 4) > 0
    first = quarter // 2
    second = quarter - 2 * first
    whole = quarter == 4
    a = jnp.where(whole, 2, jnp.where(swap, second, first))
    b = jnp.where(whole, 2, jnp.where(swap, first, second))
    return swap, a, b, (orient & 1) > 0, (orient & 2) > 0


def axis_matrix(cls, flip, halves, flip_rows):
    out = {}
    is0, is1 = cls == 0, cls == 1
    for r in range(6):
        for c in range(6):

            def entry(r0, c0):
                return jnp.where(
                    is0,
                    float(halves[0][r0, c0]),
                    jnp.where(is1, float(halves[1][r0, c0]), 1.0 if r0 == c0 else 0.0),
                )

            flipped = entry(5 - r, c) if flip_rows else entry(r, 5 - c)
            out[r, c] = jnp.where(flip, flipped, entry(r, c))
    return out


def source_matrices(quarter, orient):
    swap, a, b, flip_a, flip_b = axis_classes(quarter, orient)
    halves = TABLES["to_half"]
    return swap, axis_matrix(a, flip_a, halves, True), axis_matrix(b, flip_b, halves, True)


def target_matrices(quarter, orient):
    swap, a, b, flip_a, flip_b = axis_classes(quarter, orient)
    halves = TABLES["from_half"]
    return swap, axis_matrix(a, flip_a, halves, False), axis_matrix(b, flip_b, halves, False)


def put_matrices(ref, a, b, swap):
    for r in range(6):
        for c in range(6):
            ref[6 * r + c] = a[r, c]
            ref[36 + 6 * r + c] = b[r, c]
    ref[72] = jnp.where(swap, 1.0, 0.0)


def two_axes(x, coef, rows):
    y = {}
    for b in range(6):
        for r in range(6):
            acc = coef[6 * r, rows] * x[0, b]
            for a in range(1, 6):
                acc = acc + coef[6 * r + a, rows] * x[a, b]
            y[r, b] = acc
    z = {}
    for r in range(6):
        for s in range(6):
            acc = coef[36 + 6 * s, rows] * y[r, 0]
            for b in range(1, 6):
                acc = acc + coef[36 + 6 * s + b, rows] * y[r, b]
            z[r, s] = acc
    return z


def swapped(x, swap):
    return {
        (a, b): x[a, b] if a == b else jnp.where(swap, x[b, a], x[a, b])
        for a in range(6)
        for b in range(6)
    }


def scatter_faces(z_ref, elem_row, face_row, elems, left_ref):
    lanes = elem_row.shape[1]
    width = 2 * PAD
    for tile in range(lanes // 128):
        at = slice(tile * 128, (tile + 1) * 128)
        high, low = split(z_ref[tile * width : (tile + 1) * width, :])
        face = face_row[:, at]
        for f in range(6):
            mask = jnp.where(face == f, 1.0, 0.0).astype(BF16)
            left_ref[2 * f * width : (2 * f + 1) * width, at] = high * mask
            left_ref[(2 * f + 1) * width : (2 * f + 2) * width, at] = low * mask
    hot = one_hot(elem_row, elems)
    out = []
    for f in range(0, 6, 3):
        both = mm_nt(left_ref[2 * f * width : 2 * (f + 3) * width, :], hot)
        for g in range(3):
            out.append(both[2 * g * width : (2 * g + 1) * width] + both[(2 * g + 1) * width : (2 * g + 2) * width])
    return jnp.concatenate(out, axis=0)


def side_by_side(sums, elems):
    out = []
    for f in range(6):
        at = f * 2 * PAD
        out.append(jnp.concatenate([sums[at : at + PAD], sums[at + PAD : at + 2 * PAD]], axis=1))
    return jnp.concatenate(out, axis=0)


def zero_pad_rows(ref, blocks):
    for block in range(blocks):
        ref[block * PAD + 32 : block * PAD + 40, :] = jnp.zeros((8, 128), F32)


def both_lanes(x):
    return jnp.concatenate([x, x], axis=1)


def send_message(table_ref, slot_rows, coef_ref, xs_ref, spread_ref, out_ref, sent, first, mp=None):
    gather_faces(table_ref, as_int(slot_rows[0:1]), as_int(slot_rows[1:2]), xs_ref)
    get = spread(slot_rows, spread_ref)
    own_m = get(5)
    rows = slice(None)
    swap = coef_ref[72] > 0.5

    def load(kind):
        return {
            (a, b): xs_ref[pl.ds(kind * PAD + 6 * a + b, 2 * CHANNELS, stride=2 * PAD), :]
            for a in range(6)
            for b in range(6)
        }

    if first:
        v = two_axes(swapped(load(0), swap), coef_ref, rows)
        g = two_axes(swapped(load(1), swap), coef_ref, rows)
        for a in range(6):
            for b in range(6):
                n = 6 * a + b
                out_ref[pl.ds(n, 8, stride=FIRST), :] = v[a, b]
                out_ref[pl.ds(36 + n, 8, stride=FIRST), :] = (0.5 * PENALTY * own_m) * v[a, b] - 0.5 * g[a, b]
        for n in range(72, FIRST):
            out_ref[pl.ds(n, 8, stride=FIRST), :] = own_m
    else:
        tau = 0.5 * PENALTY * (own_m + mp)
        v, g = load(0), load(1)
        x = {key: tau * v[key] - 0.5 * g[key] for key in v}
        z = two_axes(swapped(x, swap), coef_ref, rows)
        for a in range(6):
            for b in range(6):
                out_ref[pl.ds(6 * a + b, 8, stride=36), :] = z[a, b]
    rows = out_ref.shape[0] // CHANNELS
    near_ref, far_ref, other_ref = sent
    near_ref[...] = out_ref[0:rows, :]
    for place, ref in enumerate((far_ref, other_ref)):
        ref[0:rows, :] = out_ref[(2 + place) * rows : (3 + place) * rows, :]
        ref[rows : 2 * rows, :] = out_ref[rows : 2 * rows, :]


def prepare(
    own_ref, count_ref, table_hbm, metric_hbm, field_hbm, traces_hbm,
    metric_ref, u_ref, entry_ref, partner_ref, slot_ref, counts_ref, coef_ref, near_ref, far_ref, other_ref,
    faces_ref, msg_ref, table_ref, field_ref, traces_ref, xs_ref, spread_ref, sems,
):
    pairs = (
        (table_hbm, table_ref), (metric_hbm, metric_ref), (field_hbm, field_ref), (traces_hbm, traces_ref),
    )
    copies = [
        pltpu.make_async_copy(source, target, sems.at[place])
        for place, (source, target) in enumerate(pairs)
    ]
    for copy in copies:
        copy.start()
    for copy in copies[:2]:
        copy.wait()
    elems = field_ref.shape[2]
    lanes = table_ref.shape[1]
    tiles = lanes // 128
    own = own_ref[0]
    metric = metric_ref[...]
    element, face, quarter, orient, partner, link = (table_ref[r : r + 1, :] for r in range(6))
    used = partner >= 0
    local = partner == own
    distance = partner - own
    near = 1 - 2 * (own & 1)
    far = 2 - 2 * (own & 2)
    channel = jnp.where(
        distance == near, 0, jnp.where(distance == -near, 1, jnp.where(distance == far, 2, 3))
    )
    channel = jnp.where(used & jnp.logical_not(local), channel, -1)
    m1 = metric.astype(BF16).astype(F32)
    m2 = (metric - m1).astype(BF16).astype(F32)
    m3 = metric - m1 - m2
    hot = one_hot(element, elems)
    metric_rows = mm(stack_rows([m1, m2, m3], elems).astype(BF16), hot)
    parts = [metric_rows[r : r + 1] for r in range(3)]
    att = stack_rows([element.astype(F32), face.astype(F32), quarter.astype(F32), orient.astype(F32),
                      jnp.where(used, 1.0, 0.0)] + parts, lanes)
    link_hot = one_hot(link & (CAP - 1), CAP)
    left = jnp.concatenate([jnp.where(channel == s, att, 0.0) for s in range(CHANNELS)], axis=0)
    slots = mm_nt(left.astype(BF16), link_hot)
    slots = jnp.concatenate([slots[8 * s : 8 * s + 8] for s in range(CHANNELS)], axis=1)

    def finished(rows8, n):
        total = rows8[5:6] + rows8[6:7] + rows8[7:8]
        return jnp.where(sub_iota((8, n)) == 5, total, rows8)

    slot_rows = finished(slots, CHANNELS * CAP)
    slot_ref[...] = slot_rows
    left = jnp.concatenate([att[:, t * 128 : (t + 1) * 128] for t in range(tiles)], axis=0)
    spots = mm(left.astype(BF16), link_hot)
    high_link = link // CAP
    mates = spots[0:8]
    for t in range(1, tiles):
        mates = jnp.where(high_link == t, spots[8 * t : 8 * t + 8], mates)
    mates = finished(mates, lanes)
    partner_ref[...] = mates
    entry = finished(att, lanes)
    entry = jnp.where((sub_iota((8, lanes)) == 4) & jnp.logical_not(local), 0.0, entry)
    entry_ref[...] = entry
    kinds = sub_iota((48, lanes)) == 8 * face + quarter
    counts_ref[0] = mm_nt(jnp.where(kinds & used, 1.0, 0.0).astype(BF16), hot)
    weight = jnp.where(kinds & local, mates[5:6], 0.0)
    high, low = split(weight)
    counts_ref[1] = mm_nt(high, hot) + mm_nt(low, hot)

    get = spread(slot_rows, spread_ref)
    swap, a, b = source_matrices(as_int(get(2)), as_int(get(3)))
    put_matrices(coef_ref, a, b, swap)
    for copy in copies[2:]:
        copy.wait()
    alive = lax.broadcasted_iota(I32, (1, elems), 1) < count_ref[0]
    u = jnp.concatenate([jnp.where(alive, field_ref[comp], 0.0) for comp in range(2)], axis=1)
    u_ref[...] = u
    face_tables_of(
        u, both_lanes(metric), traces_ref[...], faces_ref
    )
    sent = (near_ref, far_ref, other_ref)
    send_message(faces_ref, slot_rows, coef_ref, xs_ref, spread_ref, msg_ref, sent, True)


def local_entries(faces_ref, entry, mates, coef_ref, xs_ref, zs_ref, spread_ref, left_ref):
    lanes = entry.shape[1]
    tiles = lanes // 128
    elems = faces_ref.shape[1]
    gather_faces(faces_ref, as_int(mates[0:1]), as_int(mates[1:2]), xs_ref)
    own_m = spread(entry, spread_ref)(5)
    mate_m = spread(mates, spread_ref)(5)
    tau_all = 0.5 * PENALTY * (own_m + mate_m)
    zero_pad_rows(zs_ref, 2 * tiles)
    for group in range(2 * tiles // 8):
        rows = slice(8 * group, 8 * group + 8)
        base = 8 * group * 2 * PAD
        tau = tau_all[rows]
        swap = coef_ref[72, rows] > 0.5
        x = {}
        for a in range(6):
            for b in range(6):
                n = 6 * a + b
                v = xs_ref[pl.ds(base + n, 8, stride=2 * PAD), :]
                g = xs_ref[pl.ds(base + PAD + n, 8, stride=2 * PAD), :]
                x[a, b] = tau * v - 0.5 * g
        z = two_axes(swapped(x, swap), coef_ref, rows)
        for a in range(6):
            for b in range(6):
                zs_ref[pl.ds(8 * group * PAD + 6 * a + b, 8, stride=PAD), :] = z[a, b]
    face = jnp.where(entry[4:5] > 0.5, as_int(entry[1:2]), -1)
    return scatter_faces(zs_ref, as_int(entry[0:1]), face, elems, left_ref)


def local_first(
    near_ref, entry_ref, partner_ref, slot_ref, metric_ref, u_ref, pin_ref, counts_ref, traces_ref, rate_ref,
    near_out_ref, part_ref, coef_ref, coef_in_ref,
    faces_ref, xs_ref, zs_ref, spread_ref, left_ref,
):
    near_out_ref[...] = near_ref[...]
    face_tables_of(u_ref[...], both_lanes(metric_ref[...]), traces_ref[...], faces_ref)
    entry, mates = entry_ref[...], partner_ref[...]
    tiles = entry.shape[1] // 128
    elems = faces_ref.shape[1]
    get = spread(mates, spread_ref)
    from_quarter, from_orient = as_int(get(2)), as_int(get(3))
    get = spread(entry, spread_ref)
    to_quarter, to_orient = as_int(get(2)), as_int(get(3))
    for group in range(2 * tiles // 8):
        rows = slice(8 * group, 8 * group + 8)
        swap_in, a_in, b_in = source_matrices(from_quarter[rows], from_orient[rows])
        swap_out, a_out, b_out = target_matrices(to_quarter[rows], to_orient[rows])

        def product(left, right):
            return {
                (r, c): sum(left[r, m] * right[m, c] for m in range(6))
                for r in range(6)
                for c in range(6)
            }

        a, b = product(a_out, a_in), product(b_out, b_in)
        for r in range(6):
            for c in range(6):
                coef_ref[6 * r + c, rows] = jnp.where(swap_out, b[r, c], a[r, c])
                coef_ref[36 + 6 * r + c, rows] = jnp.where(swap_out, a[r, c], b[r, c])
        coef_ref[72, rows] = jnp.where(swap_out != swap_in, 1.0, 0.0)
    get = spread(slot_ref[...], spread_ref)
    swap, a, b = target_matrices(as_int(get(2)), as_int(get(3)))
    put_matrices(coef_in_ref, a, b, swap)
    sums = local_entries(faces_ref, entry, mates, coef_ref, xs_ref, zs_ref, spread_ref, left_ref)
    rate = known_rate(
        sums, faces_ref, counts_ref[0], counts_ref[1], metric_ref[...], u_ref[...], pin_ref[...],
        rate_ref,
    )
    part_ref[...] = u_ref[...] + TIME_STEP * rate


def arrived(swap_ref, far_ref, other_ref, all_ref):
    rows = swap_ref.shape[0] // 2
    all_ref[0 : 2 * rows, :] = swap_ref[...]
    all_ref[2 * rows : 3 * rows, :] = far_ref[0:rows, :]
    all_ref[3 * rows : 4 * rows, :] = other_ref[0:rows, :]


def land(y, slot_rows, coef_in_ref, zs_ref, elems, left_ref):
    swap = coef_in_ref[72] > 0.5
    z = swapped(two_axes(y, coef_in_ref, slice(None)), swap)
    zero_pad_rows(zs_ref, 2 * CHANNELS)
    for a in range(6):
        for b in range(6):
            zs_ref[pl.ds(6 * a + b, 2 * CHANNELS, stride=PAD), :] = z[a, b]
    face = jnp.where(slot_rows[4:5] > 0.5, as_int(slot_rows[1:2]), -1)
    sums = scatter_faces(zs_ref, as_int(slot_rows[0:1]), face, elems, left_ref)
    return side_by_side(sums, elems)


def known_rate(
    sums, faces_ref, counts, mates, metric, u, pin, rate_ref,
):
    elems = faces_ref.shape[1]
    metric2 = both_lanes(metric)
    lift = (LIFTING * metric2) * side_by_side(sums, elems)
    own = own_share(faces_ref, counts, mates, metric, elems)
    whole = 4 * 6 * PAD
    terms = jnp.concatenate([own[:whole], own[whole:] + lift, (metric2 * metric2) * u], axis=0)
    nodes = u.shape[0]
    high, low = split(terms)
    both = mm(rate_ref[...], high)
    return DIFFUSION * (both[:nodes] + both[nodes:] + mm(rate_ref[0:nodes, :], low)) - both_lanes(pin) * u


def own_share(faces_ref, counts, mates, metric, elems):
    rows = 6 * PAD
    value_w = (0.5 * PENALTY * LIFTING) * metric * (metric * counts + mates)
    deriv_w = (0.5 * LIFTING) * metric * counts

    def faces(kind, comp):
        at = (kind * 2 + comp) * rows
        return faces_ref[at : at + rows, :].astype(F32) + faces_ref[at + 4 * rows : at + 5 * rows, :].astype(F32)

    per_comp = []
    for comp in range(2):
        v, g = faces(0, comp), faces(1, comp)
        blocks = []
        for quarter in range(5):
            for f in range(6):
                at = slice(f * PAD, (f + 1) * PAD)
                row = slice(8 * f + quarter, 8 * f + quarter + 1)
                blocks.append(-(value_w[row] * v[at] + deriv_w[row] * g[at]))
        per_comp.append(jnp.concatenate(blocks, axis=0))
    return jnp.concatenate(per_comp, axis=1)


def placed(sums, metric, place_ref):
    high, low = split((LIFTING * both_lanes(metric)) * sums)
    place = place_ref[...]
    return mm(place, high) + mm(place, low)


def finish_first(
    in_swap, in_other, in_far, near_sent, far_sent, other_sent, part_ref, slot_ref, metric_ref, coef_ref, coef_in_ref,
    place_ref, traces_ref,
    u1_ref, faces1_ref, mate_ref, near_ref, far_ref, other_ref,
    msg_ref, all_ref, own_ref, xs_ref, zs_ref, spread_ref, left_ref,
):
    elems = faces1_ref.shape[1]
    metric = metric_ref[...]
    slot_rows = slot_ref[...]
    arrived(in_swap, in_far, in_other, all_ref)
    block = near_sent.shape[0]
    own_ref[0:block, :] = near_sent[...]
    own_ref[block : 2 * block, :] = far_sent[block : 2 * block, :]
    own_ref[2 * block : 3 * block, :] = far_sent[0:block, :]
    own_ref[3 * block : 4 * block, :] = other_sent[0:block, :]
    own_m = spread(slot_rows, spread_ref)(5)
    mate_m = all_ref[pl.ds(72, 8, stride=FIRST), :]
    y = {}
    for a in range(6):
        for b in range(6):
            n = 6 * a + b
            theirs, ours = all_ref[pl.ds(n, 8, stride=FIRST), :], own_ref[pl.ds(n, 8, stride=FIRST), :]
            y[a, b] = (0.5 * PENALTY) * (own_m * theirs - mate_m * ours) + all_ref[pl.ds(36 + n, 8, stride=FIRST), :]
    sums = land(y, slot_rows, coef_in_ref, zs_ref, elems, left_ref)
    mate_ref[...] = jnp.concatenate(
        [all_ref[s * block + 72 : s * block + 73, :] for s in range(CHANNELS)], axis=1
    )
    u1 = part_ref[...] + (TIME_STEP * DIFFUSION) * placed(sums, metric, place_ref)
    u1_ref[...] = u1
    face_tables_of(u1, both_lanes(metric), traces_ref[...], faces1_ref)
    sent = (near_ref, far_ref, other_ref)
    send_message(faces1_ref, slot_rows, coef_ref, xs_ref, spread_ref, msg_ref, sent, False, mate_m)


def local_second(
    near_ref, faces_ref, entry_ref, partner_ref, slot_ref, mate_ref, metric_ref, u0_ref, u_ref, pin_ref, counts_ref,
    coef_ref, rate_ref,
    near_out_ref, part_ref,
    xs_ref, zs_ref, spread_ref, left_ref,
):
    near_out_ref[...] = near_ref[...]
    elems = faces_ref.shape[1]
    sums = local_entries(
        faces_ref, entry_ref[...], partner_ref[...], coef_ref, xs_ref, zs_ref, spread_ref, left_ref
    )
    slot_rows = slot_ref[...]
    kinds = sub_iota((48, slot_rows.shape[1])) == as_int(8.0 * slot_rows[1:2] + slot_rows[2:3])
    high, low = split(jnp.where(kinds & (slot_rows[4:5] > 0.5), mate_ref[...], 0.0))
    hot = one_hot(as_int(slot_rows[0:1]), elems)
    mates = counts_ref[1] + mm_nt(high, hot) + mm_nt(low, hot)
    u = u_ref[...]
    rate = known_rate(
        sums, faces_ref, counts_ref[0], mates, metric_ref[...], u, pin_ref[...],
        rate_ref,
    )
    part_ref[...] = 0.5 * u0_ref[...] + 0.5 * (u + TIME_STEP * rate)


def finish_second(
    in_swap, in_other, in_far, part_ref, slot_ref, metric_ref, coef_in_ref, place_ref,
    out_ref,
    all_ref, zs_ref, left_ref,
):
    elems = metric_ref.shape[1]
    arrived(in_swap, in_far, in_other, all_ref)
    y = {(a, b): all_ref[pl.ds(6 * a + b, 8, stride=36), :] for a in range(6) for b in range(6)}
    sums = land(y, slot_ref[...], coef_in_ref, zs_ref, elems, left_ref)
    out = part_ref[...] + (0.5 * TIME_STEP * DIFFUSION) * placed(sums, metric_ref[...], place_ref)
    for comp in range(2):
        out_ref[comp] = out[:, comp * elems : (comp + 1) * elems]


def call(kernel, outs, scratch, *args, smem=0, copies=0):
    vmem = pl.BlockSpec(memory_space=pltpu.VMEM)
    scalar = pl.BlockSpec(memory_space=pltpu.SMEM)
    given = pl.BlockSpec(memory_space=pl.ANY) if copies else vmem
    scratch_shapes = [pltpu.VMEM(shape, dtype) for shape, dtype in scratch]
    if copies:
        scratch_shapes.append(pltpu.SemaphoreType.DMA((copies,)))
    return pl.pallas_call(
        kernel,
        out_shape=[jax.ShapeDtypeStruct(shape, dtype) for shape, dtype in outs],
        in_specs=[scalar] * smem + [given] * (len(args) - smem),
        out_specs=[vmem] * len(outs),
        scratch_shapes=scratch_shapes,
        compiler_params=pltpu.CompilerParams(vmem_limit_bytes=(53 if copies else 16) * 2**20),
        cost_estimate=pl.CostEstimate(flops=10**9, bytes_accessed=4000000, transcendentals=0),
    )(*args)


def pairings(count):
    near = [(i, i + 1) for i in range(0, count - 1, 2)]
    far = [(i, i + 2) for i in range(count - 2) if i & 2 == 0]
    other = [(i, i + 2) for i in range(count - 2) if i & 2]
    return [[*pairs, *((b, a) for a, b in pairs)] for pairs in (near, far, other)]


def cross_exchange(far, other):
    _, far_route, other_route = pairings(lax.axis_size("slab"))
    other = lax.ppermute(other, "slab", other_route)
    far = lax.ppermute(far, "slab", far_route)
    return far, other


def sibling_exchange(near, far, other):
    own = lax.axis_index("slab")
    rows = near.shape[0]
    from_other = ((own ^ (own >> 1)) & 1) == 1
    relayed = jnp.where(from_other, other[rows:], far[rows:])
    near_route = pairings(lax.axis_size("slab"))[0]
    return lax.ppermute(jnp.concatenate([near, relayed], axis=0), "slab", near_route)


def on_device(order_field, pinning, metric, elem_count, mortar_table):
    elems = order_field.shape[2]
    lanes = mortar_table.shape[1]
    own_id = lax.axis_index("slab").astype(I32).reshape(1)
    wide = 2 * elems
    rows = 6 * PAD
    slots = CHANNELS * CAP
    both = 2 * lanes // 128
    few = 2 * CHANNELS
    first_rows = few * FIRST
    second_rows = few * 36
    first_sent = [((n * first_rows // CHANNELS, 128), F32) for n in (1, 2, 2)]
    second_sent = [((n * second_rows // CHANNELS, 128), F32) for n in (1, 2, 2)]
    field_out = ((216, wide), F32)
    faces_out = ((8 * rows, elems), BF16)
    few_scratch = [((few * 2 * PAD, 128), F32), ((few * PAD, 128), F32), ((few * 8, 128), F32), ((4 * rows, slots), BF16)]
    both_scratch = [((both * 2 * PAD, 128), F32), ((both * PAD, 128), F32), ((both * 8, 128), F32), ((4 * rows, lanes), BF16)]
    traces, rate, place = (TABLES[name] for name in ("traces", "rate", "place"))
    metric_row, u0, entry, mates, slot, counts, coef_out, near, far, other = call(
        prepare,
        [
            ((1, elems), F32), field_out, ((8, lanes), F32), ((8, lanes), F32),
            ((8, slots), F32), ((2, 48, elems), F32), ((73, few, 128), F32), *first_sent,
        ],
        [
            faces_out, ((first_rows, 128), F32), (mortar_table.shape, I32), (order_field.shape, F32), (traces.shape, BF16),
            few_scratch[0], few_scratch[2],
        ],
        own_id, elem_count, mortar_table, metric.reshape(1, elems), order_field, traces,
        smem=2, copies=4,
    )
    got_far, got_other = cross_exchange(far, other)
    passed, part, coef_local, coef_in = call(
        local_first,
        [first_sent[0], field_out, ((73, both, 128), F32), ((73, few, 128), F32)],
        [faces_out, *both_scratch],
        near, entry, mates, slot, metric_row, u0, pinning, counts, traces, rate,
    )
    got_swap = sibling_exchange(passed, got_far, got_other)
    u1, faces1, mate_row, near, far, other = call(
        finish_first,
        [field_out, faces_out, ((1, slots), F32), *second_sent],
        [((second_rows, 128), F32), ((first_rows, 128), F32), ((first_rows, 128), F32), *few_scratch],
        got_swap, got_other, got_far, near, far, other, part, slot, metric_row, coef_out, coef_in,
        place, traces,
    )
    got_far, got_other = cross_exchange(far, other)
    passed, part = call(
        local_second,
        [second_sent[0], field_out],
        both_scratch,
        near, faces1, entry, mates, slot, mate_row, metric_row, u0, u1, pinning, counts, coef_local,
        rate,
    )
    got_swap = sibling_exchange(passed, got_far, got_other)
    (out,) = call(
        finish_second,
        [(order_field.shape, F32)],
        [((second_rows, 128), F32), few_scratch[1], few_scratch[3]],
        got_swap, got_other, got_far, part, slot, metric_row, coef_in, place,
    )
    return out


def solution(mesh):
    split_all = ("groups", "slab")
    return jax.shard_map(
        on_device,
        mesh=mesh,
        in_specs=(
            P(None, None, split_all), P(None, split_all), P(split_all), P(split_all), P(None, split_all),
        ),
        out_specs=P(None, None, split_all),
        check_vma=False,
    )
```

```python
import functools

import jax
import jax.numpy as jnp
import numpy as np
from jax import lax
from jax.experimental import pallas as pl
from jax.experimental.pallas import tpu as pltpu
from jax.sharding import PartitionSpec as P

CAP = 128
CHANNELS = 4
PENALTY = 18.0
LIFTING = 15.0
DIFFUSION = 0.001
TIME_STEP = 0.1
F32 = jnp.float32
BF16 = jnp.bfloat16
I32 = jnp.int32


def gll_points():
    inner_pt = np.sqrt(1.0 / 3.0 - 2.0 * np.sqrt(7.0) / 21.0)
    outer_pt = np.sqrt(1.0 / 3.0 + 2.0 * np.sqrt(7.0) / 21.0)
    return np.array([-1.0, -outer_pt, -inner_pt, inner_pt, outer_pt, 1.0])


def gll_weights(points):
    legendre = (63.0 * points**5 - 70.0 * points**3 + 15.0 * points) / 8.0
    return 2.0 / (30.0 * legendre**2)


def lagrange_matrix(points, targets):
    result = np.ones((targets.shape[0], points.shape[0]))
    for column in range(points.shape[0]):
        for other in range(points.shape[0]):
            if other != column:
                result[:, column] *= (targets - points[other]) / (points[column] - points[other])
    return result


def deriv_matrix(points):
    npoints = points.shape[0]
    factor = np.array(
        [
            np.prod([points[one] - points[other] for other in range(npoints) if other != one])
            for one in range(npoints)
        ]
    )
    result = np.zeros((npoints, npoints))
    for row_no in range(npoints):
        for col_no in range(npoints):
            if row_no != col_no:
                result[row_no, col_no] = factor[row_no] / (
                    factor[col_no] * (points[row_no] - points[col_no])
                )
        result[row_no, row_no] = -np.sum(result[row_no])
    return result


def second_matrix():
    derivative = deriv_matrix(gll_points())
    return np.array(
        [
            [np.sum(derivative[row_no, :] * derivative[:, col_no]) for col_no in range(6)]
            for row_no in range(6)
        ]
    )


def node_at(direction, along_idx, first_idx, second_idx):
    if direction == 0:
        return 36 * along_idx + 6 * first_idx + second_idx
    if direction == 1:
        return 36 * first_idx + 6 * along_idx + second_idx
    return 36 * first_idx + 6 * second_idx + along_idx


FIRST = 76
PAD = 40


def split_np(matrix):
    whole = np.asarray(matrix, np.float32)
    high = whole.astype(BF16)
    return high, (whole - high.astype(np.float32)).astype(BF16)


def constant_tables():
    points = gll_points()
    weights = gll_weights(points)
    derivative = deriv_matrix(points)
    second = second_matrix()
    lap = np.zeros((216, 216))
    for i in range(6):
        for j in range(6):
            for k in range(6):
                row = 36 * i + 6 * j + k
                for m in range(6):
                    lap[row, 36 * m + 6 * j + k] += second[i, m]
                    lap[row, 36 * i + 6 * m + k] += second[j, m]
                    lap[row, 36 * i + 6 * j + m] += second[k, m]
    value = np.zeros((6 * PAD, 216))
    normal = np.zeros((6 * PAD, 216))
    for face in range(6):
        direction, end = face // 2, 5 * (face % 2)
        sign = 1.0 if face % 2 else -1.0
        for a in range(6):
            for b in range(6):
                row = face * PAD + 6 * a + b
                value[row, node_at(direction, end, a, b)] = 1.0
                for m in range(6):
                    normal[row, node_at(direction, m, a, b)] += sign * derivative[end, m]
    to_half = [
        lagrange_matrix(points, (points - 1.0) / 2.0),
        lagrange_matrix(points, (points + 1.0) / 2.0),
    ]
    from_half = [0.5 * half.T * weights[None, :] / weights[:, None] for half in to_half]
    own = [from_half[side] @ to_half[side] for side in range(2)]
    place = value.T
    blocks = []
    for quarter in range(4):
        both = np.zeros((PAD, PAD))
        both[:36, :36] = np.kron(own[quarter // 2], own[quarter % 2])
        blocks.append(place @ np.kron(np.eye(6), both))
    blocks.append(place)
    own_place = np.concatenate(blocks, axis=1)
    return dict(
        traces=np.concatenate([value.astype(BF16), *split_np(normal)], axis=0),
        rate=np.concatenate(split_np(np.concatenate([own_place, lap], axis=1)), axis=0),
        place=place.astype(BF16),
        to_half=to_half,
        from_half=from_half,
    )


TABLES = constant_tables()


def split(x):
    high = x.astype(BF16)
    return high, (x - high.astype(F32)).astype(BF16)


def mm(a, b):
    return jnp.dot(a, b, preferred_element_type=F32)


def mm_nt(a, b):
    return lax.dot_general(a, b, (((1,), (1,)), ((), ())), preferred_element_type=F32)


def mm3(const_high, const_low, x):
    high, low = split(x)
    return mm(const_high, high) + mm(const_high, low) + mm(const_low, high)


def sub_iota(shape):
    return lax.broadcasted_iota(I32, shape, 0)


def one_hot(row, length):
    return jnp.where(sub_iota((length, row.shape[1])) == row, 1.0, 0.0).astype(BF16)


def as_int(row):
    return row.astype(I32)


def stack_rows(rows, lanes):
    at = sub_iota((8, lanes))
    out = jnp.zeros((8, lanes), F32)
    for place, row in enumerate(rows):
        out = jnp.where(at == place, row, out)
    return out


def face_tables_of(u, metric2, traces, table_ref):
    elems = u.shape[1] // 2
    high, low = split(u)
    third = 6 * PAD
    value, normal_high, normal_low = (traces[n * third : (n + 1) * third] for n in range(3))
    v_parts = (mm(value, high).astype(BF16), mm(value, low).astype(BF16))
    g = (mm(normal_high, high) + mm(normal_high, low) + mm(normal_low, high)) * metric2
    g_parts = split(g)
    rows = 6 * PAD
    for part in range(2):
        for kind, parts in enumerate((v_parts, g_parts)):
            for comp in range(2):
                at = ((part * 2 + kind) * 2 + comp) * rows
                table_ref[at : at + rows, :] = parts[part][:, comp * elems : (comp + 1) * elems]


def gather_faces(table_ref, elem_row, face_row, out_ref):
    elems = table_ref.shape[1]
    rows = 6 * PAD
    lanes = elem_row.shape[1]
    step = 256
    for start in range(0, lanes, step):
        hot = one_hot(elem_row[:, start : start + step], elems)
        got = mm(table_ref[...], hot)
        face = face_row[:, start : start + step]
        for kind in range(2):
            for comp in range(2):
                at = (kind * 2 + comp) * rows
                low_at = at + 4 * rows
                picked = got[at : at + PAD] + got[low_at : low_at + PAD]
                for f in range(1, 6):
                    mine = (
                        got[at + f * PAD : at + (f + 1) * PAD]
                        + got[low_at + f * PAD : low_at + (f + 1) * PAD]
                    )
                    picked = jnp.where(face == f, mine, picked)
                for t in range(step // 128):
                    tile = start // 128 + t
                    to = (2 * tile + comp) * 2 * PAD + kind * PAD
                    out_ref[to : to + PAD, :] = picked[:, t * 128 : (t + 1) * 128]


def spread(att, ref):
    tiles = att.shape[1] // 128
    for tile in range(tiles):
        for comp in range(2):
            at = (2 * tile + comp) * 8
            ref[at : at + 8, :] = att[:, tile * 128 : (tile + 1) * 128]

    def get(row):
        return ref[pl.ds(row, 2 * tiles, stride=8), :]

    return get


def axis_classes(quarter, orient):
    swap = (orient & 4) > 0
    first = quarter // 2
    second = quarter - 2 * first
    whole = quarter == 4
    a = jnp.where(whole, 2, jnp.where(swap, second, first))
    b = jnp.where(whole, 2, jnp.where(swap, first, second))
    return swap, a, b, (orient & 1) > 0, (orient & 2) > 0


def axis_matrix(cls, flip, halves, flip_rows):
    out = {}
    is0, is1 = cls == 0, cls == 1
    for r in range(6):
        for c in range(6):

            def entry(r0, c0):
                return jnp.where(
                    is0,
                    float(halves[0][r0, c0]),
                    jnp.where(is1, float(halves[1][r0, c0]), 1.0 if r0 == c0 else 0.0),
                )

            flipped = entry(5 - r, c) if flip_rows else entry(r, 5 - c)
            out[r, c] = jnp.where(flip, flipped, entry(r, c))
    return out


def source_matrices(quarter, orient):
    swap, a, b, flip_a, flip_b = axis_classes(quarter, orient)
    halves = TABLES["to_half"]
    return swap, axis_matrix(a, flip_a, halves, True), axis_matrix(b, flip_b, halves, True)


def target_matrices(quarter, orient):
    swap, a, b, flip_a, flip_b = axis_classes(quarter, orient)
    halves = TABLES["from_half"]
    return swap, axis_matrix(a, flip_a, halves, False), axis_matrix(b, flip_b, halves, False)


def put_matrices(ref, a, b, swap):
    for r in range(6):
        for c in range(6):
            ref[6 * r + c] = a[r, c]
            ref[36 + 6 * r + c] = b[r, c]
    ref[72] = jnp.where(swap, 1.0, 0.0)


def two_axes(x, coef, rows):
    y = {}
    for b in range(6):
        for r in range(6):
            acc = coef[6 * r, rows] * x[0, b]
            for a in range(1, 6):
                acc = acc + coef[6 * r + a, rows] * x[a, b]
            y[r, b] = acc
    z = {}
    for r in range(6):
        for s in range(6):
            acc = coef[36 + 6 * s, rows] * y[r, 0]
            for b in range(1, 6):
                acc = acc + coef[36 + 6 * s + b, rows] * y[r, b]
            z[r, s] = acc
    return z


def swapped(x, swap):
    return {
        (a, b): x[a, b] if a == b else jnp.where(swap, x[b, a], x[a, b])
        for a in range(6)
        for b in range(6)
    }


def scatter_faces(z_ref, elem_row, face_row, elems, left_ref):
    lanes = elem_row.shape[1]
    width = 2 * PAD
    for tile in range(lanes // 128):
        at = slice(tile * 128, (tile + 1) * 128)
        high, low = split(z_ref[tile * width : (tile + 1) * width, :])
        face = face_row[:, at]
        for f in range(6):
            mask = jnp.where(face == f, 1.0, 0.0).astype(BF16)
            left_ref[2 * f * width : (2 * f + 1) * width, at] = high * mask
            left_ref[(2 * f + 1) * width : (2 * f + 2) * width, at] = low * mask
    hot = one_hot(elem_row, elems)
    out = []
    for f in range(0, 6, 3):
        both = mm_nt(left_ref[2 * f * width : 2 * (f + 3) * width, :], hot)
        for g in range(3):
            out.append(both[2 * g * width : (2 * g + 1) * width] + both[(2 * g + 1) * width : (2 * g + 2) * width])
    return jnp.concatenate(out, axis=0)


def side_by_side(sums, elems):
    out = []
    for f in range(6):
        at = f * 2 * PAD
        out.append(jnp.concatenate([sums[at : at + PAD], sums[at + PAD : at + 2 * PAD]], axis=1))
    return jnp.concatenate(out, axis=0)


def zero_pad_rows(ref, blocks):
    for block in range(blocks):
        ref[block * PAD + 32 : block * PAD + 40, :] = jnp.zeros((8, 128), F32)


def both_lanes(x):
    return jnp.concatenate([x, x], axis=1)


def send_message(table_ref, slot_rows, coef_ref, xs_ref, spread_ref, out_ref, sent, first, mp=None):
    gather_faces(table_ref, as_int(slot_rows[0:1]), as_int(slot_rows[1:2]), xs_ref)
    get = spread(slot_rows, spread_ref)
    own_m = get(5)
    rows = slice(None)
    swap = coef_ref[72] > 0.5

    def load(kind):
        return {
            (a, b): xs_ref[pl.ds(kind * PAD + 6 * a + b, 2 * CHANNELS, stride=2 * PAD), :]
            for a in range(6)
            for b in range(6)
        }

    if first:
        v = two_axes(swapped(load(0), swap), coef_ref, rows)
        g = two_axes(swapped(load(1), swap), coef_ref, rows)
        for a in range(6):
            for b in range(6):
                n = 6 * a + b
                out_ref[pl.ds(n, 8, stride=FIRST), :] = v[a, b]
                out_ref[pl.ds(36 + n, 8, stride=FIRST), :] = (0.5 * PENALTY * own_m) * v[a, b] - 0.5 * g[a, b]
        for n in range(72, FIRST):
            out_ref[pl.ds(n, 8, stride=FIRST), :] = own_m
    else:
        tau = 0.5 * PENALTY * (own_m + mp)
        v, g = load(0), load(1)
        x = {key: tau * v[key] - 0.5 * g[key] for key in v}
        z = two_axes(swapped(x, swap), coef_ref, rows)
        for a in range(6):
            for b in range(6):
                out_ref[pl.ds(6 * a + b, 8, stride=36), :] = z[a, b]
    rows = out_ref.shape[0] // CHANNELS
    near_ref, far_ref, other_ref = sent
    near_ref[...] = out_ref[0:rows, :]
    for place, ref in enumerate((far_ref, other_ref)):
        ref[0:rows, :] = out_ref[(2 + place) * rows : (3 + place) * rows, :]
        ref[rows : 2 * rows, :] = out_ref[rows : 2 * rows, :]


def picked_metric(metric, hot):
    m1 = metric.astype(BF16).astype(F32)
    m2 = (metric - m1).astype(BF16).astype(F32)
    return mm(stack_rows([m1, m2, metric - m1 - m2], metric.shape[1]).astype(BF16), hot)


def entry_tables(own, table_ref, metric, entry_ref, partner_ref, counts_ref):
    elems = metric.shape[1]
    lanes = table_ref.shape[1]
    tiles = lanes // 128
    element, face, quarter, orient, partner, link = (table_ref[r : r + 1, :] for r in range(6))
    used = partner >= 0
    local = partner == own
    hot = one_hot(element, elems)
    parts = picked_metric(metric, hot)
    att = stack_rows(
        [element.astype(F32), face.astype(F32), quarter.astype(F32), orient.astype(F32), jnp.where(local, 1.0, 0.0)]
        + [parts[r : r + 1] for r in range(3)],
        lanes,
    )

    def finished(rows8):
        total = rows8[5:6] + rows8[6:7] + rows8[7:8]
        return jnp.where(sub_iota(rows8.shape) == 5, total, rows8)

    left = jnp.concatenate([att[:, t * 128 : (t + 1) * 128] for t in range(tiles)], axis=0)
    spots = mm(left.astype(BF16), one_hot(link & (CAP - 1), CAP))
    high_link = link // CAP
    mates = spots[0:8]
    for t in range(1, tiles):
        mates = jnp.where(high_link == t, spots[8 * t : 8 * t + 8], mates)
    mates = finished(mates)
    partner_ref[...] = mates
    entry_ref[...] = finished(att)
    kinds = sub_iota((48, lanes)) == 8 * face + quarter
    counts_ref[0] = mm_nt(jnp.where(kinds & used, 1.0, 0.0).astype(BF16), hot)
    high, low = split(jnp.where(kinds & local, mates[5:6], 0.0))
    counts_ref[1] = mm_nt(high, hot) + mm_nt(low, hot)


def prepare(
    own_ref, count_ref, table_hbm, metric_hbm, field_hbm, traces_hbm,
    metric_ref, table_ref, u_ref, slot_ref, coef_ref, near_ref, far_ref, other_ref,
    faces_ref, msg_ref, field_ref, traces_ref, xs_ref, spread_ref, sems,
):
    pairs = (
        (table_hbm, table_ref), (metric_hbm, metric_ref), (field_hbm, field_ref), (traces_hbm, traces_ref),
    )
    copies = [
        pltpu.make_async_copy(source, target, sems.at[place])
        for place, (source, target) in enumerate(pairs)
    ]
    for copy in copies:
        copy.start()
    for copy in copies[:2]:
        copy.wait()
    elems = field_ref.shape[2]
    lanes = table_ref.shape[1]
    own = own_ref[0]
    metric = metric_ref[...]
    element, face, quarter, orient, partner, link = (table_ref[r : r + 1, :] for r in range(6))
    used = partner >= 0
    local = partner == own
    distance = partner - own
    near = 1 - 2 * (own & 1)
    far = 2 - 2 * (own & 2)
    channel = jnp.where(
        distance == near, 0, jnp.where(distance == -near, 1, jnp.where(distance == far, 2, 3))
    )
    channel = jnp.where(used & jnp.logical_not(local), channel, -1)
    att = stack_rows(
        [element.astype(F32), face.astype(F32), quarter.astype(F32), orient.astype(F32), jnp.where(used, 1.0, 0.0)],
        lanes,
    )
    link_hot = one_hot(link & (CAP - 1), CAP)
    left = jnp.concatenate([jnp.where(channel == s, att, 0.0) for s in range(CHANNELS)], axis=0)
    slots = mm_nt(left.astype(BF16), link_hot)
    slots = jnp.concatenate([slots[8 * s : 8 * s + 8] for s in range(CHANNELS)], axis=1)
    metrics = picked_metric(metric, one_hot(as_int(slots[0:1]), elems))
    slot_rows = jnp.where(sub_iota(slots.shape) == 5, metrics[0:1] + metrics[1:2] + metrics[2:3], slots)
    slot_ref[...] = slot_rows

    get = spread(slot_rows, spread_ref)
    swap, a, b = source_matrices(as_int(get(2)), as_int(get(3)))
    put_matrices(coef_ref, a, b, swap)
    for copy in copies[2:]:
        copy.wait()
    alive = lax.broadcasted_iota(I32, (1, elems), 1) < count_ref[0]
    u = jnp.concatenate([jnp.where(alive, field_ref[comp], 0.0) for comp in range(2)], axis=1)
    u_ref[...] = u
    face_tables_of(
        u, both_lanes(metric), traces_ref[...], faces_ref
    )
    sent = (near_ref, far_ref, other_ref)
    send_message(faces_ref, slot_rows, coef_ref, xs_ref, spread_ref, msg_ref, sent, True)


def local_entries(faces_ref, entry, mates, coef_ref, xs_ref, zs_ref, spread_ref, left_ref):
    lanes = entry.shape[1]
    tiles = lanes // 128
    elems = faces_ref.shape[1]
    gather_faces(faces_ref, as_int(mates[0:1]), as_int(mates[1:2]), xs_ref)
    own_m = spread(entry, spread_ref)(5)
    mate_m = spread(mates, spread_ref)(5)
    tau_all = 0.5 * PENALTY * (own_m + mate_m)
    zero_pad_rows(zs_ref, 2 * tiles)
    for group in range(2 * tiles // 8):
        rows = slice(8 * group, 8 * group + 8)
        base = 8 * group * 2 * PAD
        tau = tau_all[rows]
        swap = coef_ref[72, rows] > 0.5
        x = {}
        for a in range(6):
            for b in range(6):
                n = 6 * a + b
                v = xs_ref[pl.ds(base + n, 8, stride=2 * PAD), :]
                g = xs_ref[pl.ds(base + PAD + n, 8, stride=2 * PAD), :]
                x[a, b] = tau * v - 0.5 * g
        z = two_axes(swapped(x, swap), coef_ref, rows)
        for a in range(6):
            for b in range(6):
                zs_ref[pl.ds(8 * group * PAD + 6 * a + b, 8, stride=PAD), :] = z[a, b]
    face = jnp.where(entry[4:5] > 0.5, as_int(entry[1:2]), -1)
    return scatter_faces(zs_ref, as_int(entry[0:1]), face, elems, left_ref)


def local_first(
    own_ref, near_ref, table_ref, slot_ref, metric_ref, u_ref, pin_ref, traces_ref, rate_ref,
    near_out_ref, part_ref, entry_ref, partner_ref, counts_ref, coef_ref, coef_in_ref,
    faces_ref, xs_ref, zs_ref, spread_ref, left_ref,
):
    near_out_ref[...] = near_ref[...]
    face_tables_of(u_ref[...], both_lanes(metric_ref[...]), traces_ref[...], faces_ref)
    entry_tables(own_ref[0], table_ref, metric_ref[...], entry_ref, partner_ref, counts_ref)
    entry, mates = entry_ref[...], partner_ref[...]
    tiles = entry.shape[1] // 128
    elems = faces_ref.shape[1]
    get = spread(mates, spread_ref)
    from_quarter, from_orient = as_int(get(2)), as_int(get(3))
    get = spread(entry, spread_ref)
    to_quarter, to_orient = as_int(get(2)), as_int(get(3))
    for group in range(2 * tiles // 8):
        rows = slice(8 * group, 8 * group + 8)
        swap_in, a_in, b_in = source_matrices(from_quarter[rows], from_orient[rows])
        swap_out, a_out, b_out = target_matrices(to_quarter[rows], to_orient[rows])

        def product(left, right):
            return {
                (r, c): sum(left[r, m] * right[m, c] for m in range(6))
                for r in range(6)
                for c in range(6)
            }

        a, b = product(a_out, a_in), product(b_out, b_in)
        for r in range(6):
            for c in range(6):
                coef_ref[6 * r + c, rows] = jnp.where(swap_out, b[r, c], a[r, c])
                coef_ref[36 + 6 * r + c, rows] = jnp.where(swap_out, a[r, c], b[r, c])
        coef_ref[72, rows] = jnp.where(swap_out != swap_in, 1.0, 0.0)
    get = spread(slot_ref[...], spread_ref)
    swap, a, b = target_matrices(as_int(get(2)), as_int(get(3)))
    put_matrices(coef_in_ref, a, b, swap)
    sums = local_entries(faces_ref, entry, mates, coef_ref, xs_ref, zs_ref, spread_ref, left_ref)
    rate = known_rate(
        sums, faces_ref, counts_ref[0], counts_ref[1], metric_ref[...], u_ref[...], pin_ref[...],
        rate_ref,
    )
    part_ref[...] = u_ref[...] + TIME_STEP * rate


def arrived(swap_ref, far_ref, other_ref, all_ref):
    rows = swap_ref.shape[0] // 2
    all_ref[0 : 2 * rows, :] = swap_ref[...]
    all_ref[2 * rows : 3 * rows, :] = far_ref[0:rows, :]
    all_ref[3 * rows : 4 * rows, :] = other_ref[0:rows, :]


def land(y, slot_rows, coef_in_ref, zs_ref, elems, left_ref, first):
    rows = slice(2 * first, 2 * first + 4)
    slot_rows = slot_rows[:, first * CAP : (first + 2) * CAP]
    swap = coef_in_ref[72, rows] > 0.5
    z = swapped(two_axes(y, coef_in_ref, rows), swap)
    zero_pad_rows(zs_ref, 4)
    for a in range(6):
        for b in range(6):
            zs_ref[pl.ds(6 * a + b, 4, stride=PAD), :] = z[a, b]
    face = jnp.where(slot_rows[4:5] > 0.5, as_int(slot_rows[1:2]), -1)
    sums = scatter_faces(zs_ref, as_int(slot_rows[0:1]), face, elems, left_ref)
    return side_by_side(sums, elems)


def first_terms(theirs_ref, ours_ref, own_m):
    mate_m = theirs_ref[pl.ds(72, 4, stride=FIRST), :]
    y = {}
    for a in range(6):
        for b in range(6):
            n = 6 * a + b
            theirs, ours = theirs_ref[pl.ds(n, 4, stride=FIRST), :], ours_ref[pl.ds(n, 4, stride=FIRST), :]
            y[a, b] = (0.5 * PENALTY) * (own_m * theirs - mate_m * ours) + theirs_ref[pl.ds(36 + n, 4, stride=FIRST), :]
    return y


def land_first(
    in_other, in_far, far_sent, other_sent, part_ref, slot_ref, metric_ref, coef_in_ref, place_ref,
    out_ref,
    theirs_ref, ours_ref, zs_ref, spread_ref, left_ref,
):
    block = in_far.shape[0] // 2
    for place, (got, sent) in enumerate(((in_far, far_sent), (in_other, other_sent))):
        theirs_ref[place * block : (place + 1) * block, :] = got[0:block, :]
        ours_ref[place * block : (place + 1) * block, :] = sent[0:block, :]
    slot_rows = slot_ref[...]
    own_m = spread(slot_rows, spread_ref)(5)
    y = first_terms(theirs_ref, ours_ref, own_m[4:8])
    sums = land(y, slot_rows, coef_in_ref, zs_ref, metric_ref.shape[1], left_ref, 2)
    out_ref[...] = part_ref[...] + (TIME_STEP * DIFFUSION) * placed(sums, metric_ref[...], place_ref)


def land_second(
    in_other, in_far, part_ref, slot_ref, metric_ref, coef_in_ref, place_ref,
    out_ref,
    theirs_ref, zs_ref, left_ref,
):
    block = in_far.shape[0] // 2
    theirs_ref[0:block, :] = in_far[0:block, :]
    theirs_ref[block : 2 * block, :] = in_other[0:block, :]
    y = {(a, b): theirs_ref[pl.ds(6 * a + b, 4, stride=36), :] for a in range(6) for b in range(6)}
    sums = land(y, slot_ref[...], coef_in_ref, zs_ref, metric_ref.shape[1], left_ref, 2)
    out_ref[...] = part_ref[...] + (0.5 * TIME_STEP * DIFFUSION) * placed(sums, metric_ref[...], place_ref)


def known_rate(
    sums, faces_ref, counts, mates, metric, u, pin, rate_ref,
):
    elems = faces_ref.shape[1]
    metric2 = both_lanes(metric)
    lift = (LIFTING * metric2) * side_by_side(sums, elems)
    own = own_share(faces_ref, counts, mates, metric, elems)
    whole = 4 * 6 * PAD
    terms = jnp.concatenate([own[:whole], own[whole:] + lift, (metric2 * metric2) * u], axis=0)
    nodes = u.shape[0]
    high, low = split(terms)
    both = mm(rate_ref[...], high)
    return DIFFUSION * (both[:nodes] + both[nodes:] + mm(rate_ref[0:nodes, :], low)) - both_lanes(pin) * u


def own_share(faces_ref, counts, mates, metric, elems):
    rows = 6 * PAD
    value_w = (0.5 * PENALTY * LIFTING) * metric * (metric * counts + mates)
    deriv_w = (0.5 * LIFTING) * metric * counts

    def faces(kind, comp):
        at = (kind * 2 + comp) * rows
        return faces_ref[at : at + rows, :].astype(F32) + faces_ref[at + 4 * rows : at + 5 * rows, :].astype(F32)

    per_comp = []
    for comp in range(2):
        v, g = faces(0, comp), faces(1, comp)
        blocks = []
        for quarter in range(5):
            for f in range(6):
                at = slice(f * PAD, (f + 1) * PAD)
                row = slice(8 * f + quarter, 8 * f + quarter + 1)
                blocks.append(-(value_w[row] * v[at] + deriv_w[row] * g[at]))
        per_comp.append(jnp.concatenate(blocks, axis=0))
    return jnp.concatenate(per_comp, axis=1)


def placed(sums, metric, place_ref):
    high, low = split((LIFTING * both_lanes(metric)) * sums)
    place = place_ref[...]
    return mm(place, high) + mm(place, low)


def finish_first(
    in_swap, in_other, in_far, near_sent, far_sent, part_ref, slot_ref, metric_ref, coef_ref, coef_in_ref,
    place_ref, traces_ref,
    u1_ref, faces1_ref, mate_ref, near_ref, far_ref, other_ref,
    msg_ref, all_ref, own_ref, xs_ref, zs_ref, spread_ref, left_ref,
):
    elems = faces1_ref.shape[1]
    metric = metric_ref[...]
    slot_rows = slot_ref[...]
    arrived(in_swap, in_far, in_other, all_ref)
    block = near_sent.shape[0]
    own_ref[0:block, :] = near_sent[...]
    own_ref[block : 2 * block, :] = far_sent[block : 2 * block, :]
    own_m = spread(slot_rows, spread_ref)(5)
    mate_m = all_ref[pl.ds(72, 8, stride=FIRST), :]
    y = first_terms(all_ref, own_ref, own_m[0:4])
    sums = land(y, slot_rows, coef_in_ref, zs_ref, elems, left_ref, 0)
    mate_ref[...] = jnp.concatenate(
        [all_ref[s * block + 72 : s * block + 73, :] for s in range(CHANNELS)], axis=1
    )
    u1 = part_ref[...] + (TIME_STEP * DIFFUSION) * placed(sums, metric, place_ref)
    u1_ref[...] = u1
    face_tables_of(u1, both_lanes(metric), traces_ref[...], faces1_ref)
    sent = (near_ref, far_ref, other_ref)
    send_message(faces1_ref, slot_rows, coef_ref, xs_ref, spread_ref, msg_ref, sent, False, mate_m)


def local_second(
    near_ref, faces_ref, entry_ref, partner_ref, slot_ref, mate_ref, metric_ref, u0_ref, u_ref, pin_ref, counts_ref,
    coef_ref, rate_ref,
    near_out_ref, part_ref,
    xs_ref, zs_ref, spread_ref, left_ref,
):
    near_out_ref[...] = near_ref[...]
    elems = faces_ref.shape[1]
    sums = local_entries(
        faces_ref, entry_ref[...], partner_ref[...], coef_ref, xs_ref, zs_ref, spread_ref, left_ref
    )
    slot_rows = slot_ref[...]
    kinds = sub_iota((48, slot_rows.shape[1])) == as_int(8.0 * slot_rows[1:2] + slot_rows[2:3])
    high, low = split(jnp.where(kinds & (slot_rows[4:5] > 0.5), mate_ref[...], 0.0))
    hot = one_hot(as_int(slot_rows[0:1]), elems)
    mates = counts_ref[1] + mm_nt(high, hot) + mm_nt(low, hot)
    u = u_ref[...]
    rate = known_rate(
        sums, faces_ref, counts_ref[0], mates, metric_ref[...], u, pin_ref[...],
        rate_ref,
    )
    part_ref[...] = 0.5 * u0_ref[...] + 0.5 * (u + TIME_STEP * rate)


def finish_second(
    in_swap, part_ref, slot_ref, metric_ref, coef_in_ref, place_ref,
    out_ref,
    zs_ref, left_ref,
):
    elems = metric_ref.shape[1]
    y = {(a, b): in_swap[pl.ds(6 * a + b, 4, stride=36), :] for a in range(6) for b in range(6)}
    sums = land(y, slot_ref[...], coef_in_ref, zs_ref, elems, left_ref, 0)
    out = part_ref[...] + (0.5 * TIME_STEP * DIFFUSION) * placed(sums, metric_ref[...], place_ref)
    for comp in range(2):
        out_ref[comp] = out[:, comp * elems : (comp + 1) * elems]


def call(kernel, outs, scratch, *args, smem=0, copies=0):
    vmem = pl.BlockSpec(memory_space=pltpu.VMEM)
    scalar = pl.BlockSpec(memory_space=pltpu.SMEM)
    given = pl.BlockSpec(memory_space=pl.ANY) if copies else vmem
    scratch_shapes = [pltpu.VMEM(shape, dtype) for shape, dtype in scratch]
    if copies:
        scratch_shapes.append(pltpu.SemaphoreType.DMA((copies,)))
    return pl.pallas_call(
        kernel,
        out_shape=[jax.ShapeDtypeStruct(shape, dtype) for shape, dtype in outs],
        in_specs=[scalar] * smem + [given] * (len(args) - smem),
        out_specs=[vmem] * len(outs),
        scratch_shapes=scratch_shapes,
        compiler_params=pltpu.CompilerParams(vmem_limit_bytes=(53 if copies else 16) * 2**20),
        cost_estimate=pl.CostEstimate(flops=10**9, bytes_accessed=4000000, transcendentals=0),
    )(*args)


def pairings(count):
    near = [(i, i + 1) for i in range(0, count - 1, 2)]
    far = [(i, i + 2) for i in range(count - 2) if i & 2 == 0]
    other = [(i, i + 2) for i in range(count - 2) if i & 2]
    return [[*pairs, *((b, a) for a, b in pairs)] for pairs in (near, far, other)]


def cross_exchange(far, other):
    _, far_route, other_route = pairings(lax.axis_size("slab"))
    other = lax.ppermute(other, "slab", other_route)
    far = lax.ppermute(far, "slab", far_route)
    return far, other


def sibling_exchange(near, far, other):
    own = lax.axis_index("slab")
    rows = near.shape[0]
    from_other = ((own ^ (own >> 1)) & 1) == 1
    relayed = jnp.where(from_other, other[rows:], far[rows:])
    near_route = pairings(lax.axis_size("slab"))[0]
    return lax.ppermute(jnp.concatenate([near, relayed], axis=0), "slab", near_route)


def on_device(order_field, pinning, metric, elem_count, mortar_table):
    elems = order_field.shape[2]
    lanes = mortar_table.shape[1]
    own_id = lax.axis_index("slab").astype(I32).reshape(1)
    wide = 2 * elems
    rows = 6 * PAD
    slots = CHANNELS * CAP
    both = 2 * lanes // 128
    few = 2 * CHANNELS
    first_rows = few * FIRST
    second_rows = few * 36
    first_sent = [((n * first_rows // CHANNELS, 128), F32) for n in (1, 2, 2)]
    second_sent = [((n * second_rows // CHANNELS, 128), F32) for n in (1, 2, 2)]
    field_out = ((216, wide), F32)
    faces_out = ((8 * rows, elems), BF16)
    few_scratch = [((few * 2 * PAD, 128), F32), ((4 * PAD, 128), F32), ((few * 8, 128), F32), ((4 * rows, 2 * CAP), BF16)]
    both_scratch = [((both * 2 * PAD, 128), F32), ((both * PAD, 128), F32), ((both * 8, 128), F32), ((4 * rows, lanes), BF16)]
    traces, rate, place = (TABLES[name] for name in ("traces", "rate", "place"))
    metric_row, table, u0, slot, coef_out, near, far, other = call(
        prepare,
        [
            ((1, elems), F32), (mortar_table.shape, I32), field_out, ((8, slots), F32), ((73, few, 128), F32), *first_sent,
        ],
        [
            faces_out, ((first_rows, 128), F32), (order_field.shape, F32), (traces.shape, BF16),
            few_scratch[0], few_scratch[2],
        ],
        own_id, elem_count, mortar_table, metric.reshape(1, elems), order_field, traces,
        smem=2, copies=4,
    )
    got_far, got_other = cross_exchange(far, other)
    passed, part, entry, mates, counts, coef_local, coef_in = call(
        local_first,
        [
            first_sent[0], field_out, ((8, lanes), F32), ((8, lanes), F32), ((2, 48, elems), F32),
            ((73, both, 128), F32), ((73, few, 128), F32),
        ],
        [faces_out, *both_scratch],
        own_id, near, table, slot, metric_row, u0, pinning, traces, rate,
        smem=1,
    )
    got_swap = sibling_exchange(passed, got_far, got_other)
    (landed,) = call(
        land_first,
        [field_out],
        [((first_rows // 2, 128), F32), ((first_rows // 2, 128), F32), *few_scratch[1:]],
        got_other, got_far, far, other, part, slot, metric_row, coef_in, place,
    )
    u1, faces1, mate_row, near, far, other = call(
        finish_first,
        [field_out, faces_out, ((1, slots), F32), *second_sent],
        [((second_rows, 128), F32), ((first_rows, 128), F32), ((first_rows, 128), F32), *few_scratch],
        got_swap, got_other, got_far, near, far, landed, slot, metric_row, coef_out, coef_in,
        place, traces,
    )
    got_far, got_other = cross_exchange(far, other)
    passed, part = call(
        local_second,
        [second_sent[0], field_out],
        both_scratch,
        near, faces1, entry, mates, slot, mate_row, metric_row, u0, u1, pinning, counts, coef_local,
        rate,
    )
    got_swap = sibling_exchange(passed, got_far, got_other)
    (landed,) = call(
        land_second,
        [field_out],
        [((second_rows // 2, 128), F32), few_scratch[1], few_scratch[3]],
        got_other, got_far, part, slot, metric_row, coef_in, place,
    )
    (out,) = call(
        finish_second,
        [(order_field.shape, F32)],
        [few_scratch[1], few_scratch[3]],
        got_swap, landed, slot, metric_row, coef_in, place,
    )
    return out


def solution(mesh):
    split_all = ("groups", "slab")
    return jax.shard_map(
        on_device,
        mesh=mesh,
        in_specs=(
            P(None, None, split_all), P(None, split_all), P(split_all), P(split_all), P(None, split_all),
        ),
        out_specs=P(None, None, split_all),
        check_vma=False,
    )
```

```python
import functools

import jax
import jax.numpy as jnp
import numpy as np
from jax import lax
from jax.experimental import pallas as pl
from jax.experimental.pallas import tpu as pltpu
from jax.sharding import PartitionSpec as P

CAP = 128
CHANNELS = 4
PENALTY = 18.0
LIFTING = 15.0
DIFFUSION = 0.001
TIME_STEP = 0.1
F32 = jnp.float32
BF16 = jnp.bfloat16
I32 = jnp.int32


def gll_points():
    inner_pt = np.sqrt(1.0 / 3.0 - 2.0 * np.sqrt(7.0) / 21.0)
    outer_pt = np.sqrt(1.0 / 3.0 + 2.0 * np.sqrt(7.0) / 21.0)
    return np.array([-1.0, -outer_pt, -inner_pt, inner_pt, outer_pt, 1.0])


def gll_weights(points):
    legendre = (63.0 * points**5 - 70.0 * points**3 + 15.0 * points) / 8.0
    return 2.0 / (30.0 * legendre**2)


def lagrange_matrix(points, targets):
    result = np.ones((targets.shape[0], points.shape[0]))
    for column in range(points.shape[0]):
        for other in range(points.shape[0]):
            if other != column:
                result[:, column] *= (targets - points[other]) / (points[column] - points[other])
    return result


def deriv_matrix(points):
    npoints = points.shape[0]
    factor = np.array(
        [
            np.prod([points[one] - points[other] for other in range(npoints) if other != one])
            for one in range(npoints)
        ]
    )
    result = np.zeros((npoints, npoints))
    for row_no in range(npoints):
        for col_no in range(npoints):
            if row_no != col_no:
                result[row_no, col_no] = factor[row_no] / (
                    factor[col_no] * (points[row_no] - points[col_no])
                )
        result[row_no, row_no] = -np.sum(result[row_no])
    return result


def second_matrix():
    derivative = deriv_matrix(gll_points())
    return np.array(
        [
            [np.sum(derivative[row_no, :] * derivative[:, col_no]) for col_no in range(6)]
            for row_no in range(6)
        ]
    )


def node_at(direction, along_idx, first_idx, second_idx):
    if direction == 0:
        return 36 * along_idx + 6 * first_idx + second_idx
    if direction == 1:
        return 36 * first_idx + 6 * along_idx + second_idx
    return 36 * first_idx + 6 * second_idx + along_idx


FIRST = 73
PAD = 40


def split_np(matrix):
    whole = np.asarray(matrix, np.float32)
    high = whole.astype(BF16)
    return high, (whole - high.astype(np.float32)).astype(BF16)


def constant_tables():
    points = gll_points()
    weights = gll_weights(points)
    derivative = deriv_matrix(points)
    second = second_matrix()
    lap = np.zeros((216, 216))
    for i in range(6):
        for j in range(6):
            for k in range(6):
                row = 36 * i + 6 * j + k
                for m in range(6):
                    lap[row, 36 * m + 6 * j + k] += second[i, m]
                    lap[row, 36 * i + 6 * m + k] += second[j, m]
                    lap[row, 36 * i + 6 * j + m] += second[k, m]
    value = np.zeros((6 * PAD, 216))
    normal = np.zeros((6 * PAD, 216))
    for face in range(6):
        direction, end = face // 2, 5 * (face % 2)
        sign = 1.0 if face % 2 else -1.0
        for a in range(6):
            for b in range(6):
                row = face * PAD + 6 * a + b
                value[row, node_at(direction, end, a, b)] = 1.0
                for m in range(6):
                    normal[row, node_at(direction, m, a, b)] += sign * derivative[end, m]
    to_half = [
        lagrange_matrix(points, (points - 1.0) / 2.0),
        lagrange_matrix(points, (points + 1.0) / 2.0),
    ]
    from_half = [0.5 * half.T * weights[None, :] / weights[:, None] for half in to_half]
    own = [from_half[side] @ to_half[side] for side in range(2)]
    place = value.T
    blocks = []
    for quarter in range(4):
        both = np.zeros((PAD, PAD))
        both[:36, :36] = np.kron(own[quarter // 2], own[quarter % 2])
        blocks.append(place @ np.kron(np.eye(6), both))
    blocks.append(place)
    own_place = np.concatenate(blocks, axis=1)
    return dict(
        traces=np.concatenate([value.astype(BF16), *split_np(normal)], axis=0),
        rate=np.concatenate(split_np(np.concatenate([own_place, lap], axis=1)), axis=0),
        place=place.astype(BF16),
        to_half=to_half,
        from_half=from_half,
    )


TABLES = constant_tables()


def split(x):
    high = x.astype(BF16)
    return high, (x - high.astype(F32)).astype(BF16)


def mm(a, b):
    return jnp.dot(a, b, preferred_element_type=F32)


def mm_nt(a, b):
    return lax.dot_general(a, b, (((1,), (1,)), ((), ())), preferred_element_type=F32)


def mm3(const_high, const_low, x):
    high, low = split(x)
    return mm(const_high, high) + mm(const_high, low) + mm(const_low, high)


def sub_iota(shape):
    return lax.broadcasted_iota(I32, shape, 0)


def one_hot(row, length):
    return jnp.where(sub_iota((length, row.shape[1])) == row, 1.0, 0.0).astype(BF16)


def as_int(row):
    return row.astype(I32)


def stack_rows(rows, lanes):
    at = sub_iota((8, lanes))
    out = jnp.zeros((8, lanes), F32)
    for place, row in enumerate(rows):
        out = jnp.where(at == place, row, out)
    return out


def face_tables_of(u, metric2, traces, table_ref):
    elems = u.shape[1] // 2
    high, low = split(u)
    third = 6 * PAD
    value, normal_high, normal_low = (traces[n * third : (n + 1) * third] for n in range(3))
    v_parts = (mm(value, high).astype(BF16), mm(value, low).astype(BF16))
    g = (mm(normal_high, high) + mm(normal_high, low) + mm(normal_low, high)) * metric2
    g_parts = split(g)
    rows = 6 * PAD
    for part in range(2):
        for kind, parts in enumerate((v_parts, g_parts)):
            for comp in range(2):
                at = ((part * 2 + kind) * 2 + comp) * rows
                table_ref[at : at + rows, :] = parts[part][:, comp * elems : (comp + 1) * elems]


def gather_faces(table_ref, elem_row, face_row, out_ref):
    elems = table_ref.shape[1]
    rows = 6 * PAD
    lanes = elem_row.shape[1]
    step = 256
    for start in range(0, lanes, step):
        hot = one_hot(elem_row[:, start : start + step], elems)
        got = mm(table_ref[...], hot)
        face = face_row[:, start : start + step]
        for kind in range(2):
            for comp in range(2):
                at = (kind * 2 + comp) * rows
                low_at = at + 4 * rows
                picked = got[at : at + PAD] + got[low_at : low_at + PAD]
                for f in range(1, 6):
                    mine = (
                        got[at + f * PAD : at + (f + 1) * PAD]
                        + got[low_at + f * PAD : low_at + (f + 1) * PAD]
                    )
                    picked = jnp.where(face == f, mine, picked)
                for t in range(step // 128):
                    tile = start // 128 + t
                    to = (2 * tile + comp) * 2 * PAD + kind * PAD
                    out_ref[to : to + PAD, :] = picked[:, t * 128 : (t + 1) * 128]


def spread(att, ref):
    tiles = att.shape[1] // 128
    for tile in range(tiles):
        for comp in range(2):
            at = (2 * tile + comp) * 8
            ref[at : at + 8, :] = att[:, tile * 128 : (tile + 1) * 128]

    def get(row):
        return ref[pl.ds(row, 2 * tiles, stride=8), :]

    return get


def axis_classes(quarter, orient):
    swap = (orient & 4) > 0
    first = quarter // 2
    second = quarter - 2 * first
    whole = quarter == 4
    a = jnp.where(whole, 2, jnp.where(swap, second, first))
    b = jnp.where(whole, 2, jnp.where(swap, first, second))
    return swap, a, b, (orient & 1) > 0, (orient & 2) > 0


def axis_matrix(cls, flip, halves, flip_rows):
    out = {}
    is0, is1 = cls == 0, cls == 1
    for r in range(6):
        for c in range(6):

            def entry(r0, c0):
                return jnp.where(
                    is0,
                    float(halves[0][r0, c0]),
                    jnp.where(is1, float(halves[1][r0, c0]), 1.0 if r0 == c0 else 0.0),
                )

            flipped = entry(5 - r, c) if flip_rows else entry(r, 5 - c)
            out[r, c] = jnp.where(flip, flipped, entry(r, c))
    return out


def source_matrices(quarter, orient):
    swap, a, b, flip_a, flip_b = axis_classes(quarter, orient)
    halves = TABLES["to_half"]
    return swap, axis_matrix(a, flip_a, halves, True), axis_matrix(b, flip_b, halves, True)


def target_matrices(quarter, orient):
    swap, a, b, flip_a, flip_b = axis_classes(quarter, orient)
    halves = TABLES["from_half"]
    return swap, axis_matrix(a, flip_a, halves, False), axis_matrix(b, flip_b, halves, False)


def put_matrices(ref, a, b, swap):
    for r in range(6):
        for c in range(6):
            ref[6 * r + c] = a[r, c]
            ref[36 + 6 * r + c] = b[r, c]
    ref[72] = jnp.where(swap, 1.0, 0.0)


def two_axes(x, coef, rows):
    y = {}
    for b in range(6):
        for r in range(6):
            acc = coef[6 * r, rows] * x[0, b]
            for a in range(1, 6):
                acc = acc + coef[6 * r + a, rows] * x[a, b]
            y[r, b] = acc
    z = {}
    for r in range(6):
        for s in range(6):
            acc = coef[36 + 6 * s, rows] * y[r, 0]
            for b in range(1, 6):
                acc = acc + coef[36 + 6 * s + b, rows] * y[r, b]
            z[r, s] = acc
    return z


def swapped(x, swap):
    return {
        (a, b): x[a, b] if a == b else jnp.where(swap, x[b, a], x[a, b])
        for a in range(6)
        for b in range(6)
    }


def scatter_faces(z_ref, elem_row, face_row, elems, left_ref):
    lanes = elem_row.shape[1]
    width = 2 * PAD
    for tile in range(lanes // 128):
        at = slice(tile * 128, (tile + 1) * 128)
        high, low = split(z_ref[tile * width : (tile + 1) * width, :])
        face = face_row[:, at]
        for f in range(6):
            mask = jnp.where(face == f, 1.0, 0.0).astype(BF16)
            left_ref[2 * f * width : (2 * f + 1) * width, at] = high * mask
            left_ref[(2 * f + 1) * width : (2 * f + 2) * width, at] = low * mask
    hot = one_hot(elem_row, elems)
    out = []
    for f in range(0, 6, 3):
        both = mm_nt(left_ref[2 * f * width : 2 * (f + 3) * width, :], hot)
        for g in range(3):
            out.append(both[2 * g * width : (2 * g + 1) * width] + both[(2 * g + 1) * width : (2 * g + 2) * width])
    return jnp.concatenate(out, axis=0)


def side_by_side(sums, elems):
    out = []
    for f in range(6):
        at = f * 2 * PAD
        out.append(jnp.concatenate([sums[at : at + PAD], sums[at + PAD : at + 2 * PAD]], axis=1))
    return jnp.concatenate(out, axis=0)


def zero_pad_rows(ref, blocks):
    for block in range(blocks):
        ref[block * PAD + 32 : block * PAD + 40, :] = jnp.zeros((8, 128), F32)


def both_lanes(x):
    return jnp.concatenate([x, x], axis=1)


def send_message(table_ref, slot_rows, coef_ref, xs_ref, spread_ref, out_ref, sent, first, mp=None):
    gather_faces(table_ref, as_int(slot_rows[0:1]), as_int(slot_rows[1:2]), xs_ref)
    get = spread(slot_rows, spread_ref)
    own_m = get(5)
    rows = slice(None)
    swap = coef_ref[72] > 0.5

    def load(kind):
        return {
            (a, b): xs_ref[pl.ds(kind * PAD + 6 * a + b, 2 * CHANNELS, stride=2 * PAD), :]
            for a in range(6)
            for b in range(6)
        }

    if first:
        v = two_axes(swapped(load(0), swap), coef_ref, rows)
        g = two_axes(swapped(load(1), swap), coef_ref, rows)
        for a in range(6):
            for b in range(6):
                n = 6 * a + b
                out_ref[pl.ds(n, 8, stride=FIRST), :] = v[a, b]
                out_ref[pl.ds(36 + n, 8, stride=FIRST), :] = (0.5 * PENALTY * own_m) * v[a, b] - 0.5 * g[a, b]
        for n in range(72, FIRST):
            out_ref[pl.ds(n, 8, stride=FIRST), :] = own_m
    else:
        tau = 0.5 * PENALTY * (own_m + mp)
        v, g = load(0), load(1)
        x = {key: tau * v[key] - 0.5 * g[key] for key in v}
        z = two_axes(swapped(x, swap), coef_ref, rows)
        for a in range(6):
            for b in range(6):
                out_ref[pl.ds(6 * a + b, 8, stride=36), :] = z[a, b]
    rows = out_ref.shape[0] // CHANNELS
    near_ref, far_ref, other_ref = sent
    near_ref[...] = out_ref[0:rows, :]
    for place, ref in enumerate((far_ref, other_ref)):
        ref[0:rows, :] = out_ref[(2 + place) * rows : (3 + place) * rows, :]
        ref[rows : 2 * rows, :] = out_ref[rows : 2 * rows, :]


def picked_metric(metric, hot):
    m1 = metric.astype(BF16).astype(F32)
    m2 = (metric - m1).astype(BF16).astype(F32)
    return mm(stack_rows([m1, m2, metric - m1 - m2], metric.shape[1]).astype(BF16), hot)


def entry_tables(own, table_ref, metric, entry_ref, partner_ref, counts_ref):
    elems = metric.shape[1]
    lanes = table_ref.shape[1]
    tiles = lanes // 128
    element, face, quarter, orient, partner, link = (table_ref[r : r + 1, :] for r in range(6))
    used = partner >= 0
    local = partner == own
    hot = one_hot(element, elems)
    parts = picked_metric(metric, hot)
    att = stack_rows(
        [element.astype(F32), face.astype(F32), quarter.astype(F32), orient.astype(F32), jnp.where(local, 1.0, 0.0)]
        + [parts[r : r + 1] for r in range(3)],
        lanes,
    )

    def finished(rows8):
        total = rows8[5:6] + rows8[6:7] + rows8[7:8]
        return jnp.where(sub_iota(rows8.shape) == 5, total, rows8)

    left = jnp.concatenate([att[:, t * 128 : (t + 1) * 128] for t in range(tiles)], axis=0)
    spots = mm(left.astype(BF16), one_hot(link & (CAP - 1), CAP))
    high_link = link // CAP
    mates = spots[0:8]
    for t in range(1, tiles):
        mates = jnp.where(high_link == t, spots[8 * t : 8 * t + 8], mates)
    mates = finished(mates)
    partner_ref[...] = mates
    entry_ref[...] = finished(att)
    kinds = sub_iota((48, lanes)) == 8 * face + quarter
    counts_ref[0] = mm_nt(jnp.where(kinds & used, 1.0, 0.0).astype(BF16), hot)
    high, low = split(jnp.where(kinds & local, mates[5:6], 0.0))
    counts_ref[1] = mm_nt(high, hot) + mm_nt(low, hot)


def prepare(
    own_ref, count_ref, table_hbm, metric_hbm, field_hbm, traces_hbm,
    metric_ref, table_ref, u_ref, slot_ref, coef_ref, near_ref, far_ref, other_ref,
    faces_ref, msg_ref, field_ref, traces_ref, xs_ref, spread_ref, sems,
):
    pairs = (
        (table_hbm, table_ref), (metric_hbm, metric_ref), (field_hbm, field_ref), (traces_hbm, traces_ref),
    )
    copies = [
        pltpu.make_async_copy(source, target, sems.at[place])
        for place, (source, target) in enumerate(pairs)
    ]
    for copy in copies:
        copy.start()
    for copy in copies[:2]:
        copy.wait()
    elems = field_ref.shape[2]
    lanes = table_ref.shape[1]
    own = own_ref[0]
    metric = metric_ref[...]
    element, face, quarter, orient, partner, link = (table_ref[r : r + 1, :] for r in range(6))
    used = partner >= 0
    local = partner == own
    distance = partner - own
    near = 1 - 2 * (own & 1)
    far = 2 - 2 * (own & 2)
    channel = jnp.where(
        distance == near, 0, jnp.where(distance == -near, 1, jnp.where(distance == far, 2, 3))
    )
    channel = jnp.where(used & jnp.logical_not(local), channel, -1)
    att = stack_rows(
        [element.astype(F32), face.astype(F32), quarter.astype(F32), orient.astype(F32), jnp.where(used, 1.0, 0.0)],
        lanes,
    )
    link_hot = one_hot(link & (CAP - 1), CAP)
    left = jnp.concatenate([jnp.where(channel == s, att, 0.0) for s in range(CHANNELS)], axis=0)
    slots = mm_nt(left.astype(BF16), link_hot)
    slots = jnp.concatenate([slots[8 * s : 8 * s + 8] for s in range(CHANNELS)], axis=1)
    metrics = picked_metric(metric, one_hot(as_int(slots[0:1]), elems))
    slot_rows = jnp.where(sub_iota(slots.shape) == 5, metrics[0:1] + metrics[1:2] + metrics[2:3], slots)
    slot_ref[...] = slot_rows

    get = spread(slot_rows, spread_ref)
    swap, a, b = source_matrices(as_int(get(2)), as_int(get(3)))
    put_matrices(coef_ref, a, b, swap)
    for copy in copies[2:]:
        copy.wait()
    alive = lax.broadcasted_iota(I32, (1, elems), 1) < count_ref[0]
    u = jnp.concatenate([jnp.where(alive, field_ref[comp], 0.0) for comp in range(2)], axis=1)
    u_ref[...] = u
    face_tables_of(
        u, both_lanes(metric), traces_ref[...], faces_ref
    )
    sent = (near_ref, far_ref, other_ref)
    send_message(faces_ref, slot_rows, coef_ref, xs_ref, spread_ref, msg_ref, sent, True)


def local_entries(faces_ref, entry, mates, coef_ref, xs_ref, zs_ref, spread_ref, left_ref):
    lanes = entry.shape[1]
    tiles = lanes // 128
    elems = faces_ref.shape[1]
    gather_faces(faces_ref, as_int(mates[0:1]), as_int(mates[1:2]), xs_ref)
    own_m = spread(entry, spread_ref)(5)
    mate_m = spread(mates, spread_ref)(5)
    tau_all = 0.5 * PENALTY * (own_m + mate_m)
    zero_pad_rows(zs_ref, 2 * tiles)
    for group in range(2 * tiles // 8):
        rows = slice(8 * group, 8 * group + 8)
        base = 8 * group * 2 * PAD
        tau = tau_all[rows]
        swap = coef_ref[72, rows] > 0.5
        x = {}
        for a in range(6):
            for b in range(6):
                n = 6 * a + b
                v = xs_ref[pl.ds(base + n, 8, stride=2 * PAD), :]
                g = xs_ref[pl.ds(base + PAD + n, 8, stride=2 * PAD), :]
                x[a, b] = tau * v - 0.5 * g
        z = two_axes(swapped(x, swap), coef_ref, rows)
        for a in range(6):
            for b in range(6):
                zs_ref[pl.ds(8 * group * PAD + 6 * a + b, 8, stride=PAD), :] = z[a, b]
    face = jnp.where(entry[4:5] > 0.5, as_int(entry[1:2]), -1)
    return scatter_faces(zs_ref, as_int(entry[0:1]), face, elems, left_ref)


def local_first(
    own_ref, near_ref, table_ref, slot_ref, metric_ref, u_ref, pin_ref, traces_ref, rate_ref,
    near_out_ref, part_ref, entry_ref, partner_ref, counts_ref, coef_ref, coef_in_ref,
    faces_ref, xs_ref, zs_ref, spread_ref, left_ref,
):
    near_out_ref[...] = near_ref[...]
    face_tables_of(u_ref[...], both_lanes(metric_ref[...]), traces_ref[...], faces_ref)
    entry_tables(own_ref[0], table_ref, metric_ref[...], entry_ref, partner_ref, counts_ref)
    entry, mates = entry_ref[...], partner_ref[...]
    tiles = entry.shape[1] // 128
    elems = faces_ref.shape[1]
    get = spread(mates, spread_ref)
    from_quarter, from_orient = as_int(get(2)), as_int(get(3))
    get = spread(entry, spread_ref)
    to_quarter, to_orient = as_int(get(2)), as_int(get(3))
    for group in range(2 * tiles // 8):
        rows = slice(8 * group, 8 * group + 8)
        swap_in, a_in, b_in = source_matrices(from_quarter[rows], from_orient[rows])
        swap_out, a_out, b_out = target_matrices(to_quarter[rows], to_orient[rows])

        def product(left, right):
            return {
                (r, c): sum(left[r, m] * right[m, c] for m in range(6))
                for r in range(6)
                for c in range(6)
            }

        a, b = product(a_out, a_in), product(b_out, b_in)
        for r in range(6):
            for c in range(6):
                coef_ref[6 * r + c, rows] = jnp.where(swap_out, b[r, c], a[r, c])
                coef_ref[36 + 6 * r + c, rows] = jnp.where(swap_out, a[r, c], b[r, c])
        coef_ref[72, rows] = jnp.where(swap_out != swap_in, 1.0, 0.0)
    get = spread(slot_ref[...], spread_ref)
    swap, a, b = target_matrices(as_int(get(2)), as_int(get(3)))
    put_matrices(coef_in_ref, a, b, swap)
    sums = local_entries(faces_ref, entry, mates, coef_ref, xs_ref, zs_ref, spread_ref, left_ref)
    rate = known_rate(
        sums, faces_ref, counts_ref[0], counts_ref[1], metric_ref[...], u_ref[...], pin_ref[...],
        rate_ref,
    )
    part_ref[...] = u_ref[...] + TIME_STEP * rate


def arrived(swap_ref, far_ref, other_ref, all_ref):
    rows = swap_ref.shape[0] // 2
    all_ref[0 : 2 * rows, :] = swap_ref[...]
    all_ref[2 * rows : 3 * rows, :] = far_ref[0:rows, :]
    all_ref[3 * rows : 4 * rows, :] = other_ref[0:rows, :]


def land(y, slot_rows, coef_in_ref, zs_ref, elems, left_ref, first):
    rows = slice(2 * first, 2 * first + 4)
    slot_rows = slot_rows[:, first * CAP : (first + 2) * CAP]
    swap = coef_in_ref[72, rows] > 0.5
    z = swapped(two_axes(y, coef_in_ref, rows), swap)
    zero_pad_rows(zs_ref, 4)
    for a in range(6):
        for b in range(6):
            zs_ref[pl.ds(6 * a + b, 4, stride=PAD), :] = z[a, b]
    face = jnp.where(slot_rows[4:5] > 0.5, as_int(slot_rows[1:2]), -1)
    sums = scatter_faces(zs_ref, as_int(slot_rows[0:1]), face, elems, left_ref)
    return side_by_side(sums, elems)


def first_terms(theirs_ref, ours_ref, own_m):
    mate_m = theirs_ref[pl.ds(72, 4, stride=FIRST), :]
    y = {}
    for a in range(6):
        for b in range(6):
            n = 6 * a + b
            theirs, ours = theirs_ref[pl.ds(n, 4, stride=FIRST), :], ours_ref[pl.ds(n, 4, stride=FIRST), :]
            y[a, b] = (0.5 * PENALTY) * (own_m * theirs - mate_m * ours) + theirs_ref[pl.ds(36 + n, 4, stride=FIRST), :]
    return y


def land_first(
    in_other, in_far, far_sent, other_sent, part_ref, slot_ref, metric_ref, coef_in_ref, place_ref,
    out_ref,
    theirs_ref, ours_ref, zs_ref, spread_ref, left_ref,
):
    block = in_far.shape[0] // 2
    for place, (got, sent) in enumerate(((in_far, far_sent), (in_other, other_sent))):
        theirs_ref[place * block : (place + 1) * block, :] = got[0:block, :]
        ours_ref[place * block : (place + 1) * block, :] = sent[0:block, :]
    slot_rows = slot_ref[...]
    own_m = spread(slot_rows, spread_ref)(5)
    y = first_terms(theirs_ref, ours_ref, own_m[4:8])
    sums = land(y, slot_rows, coef_in_ref, zs_ref, metric_ref.shape[1], left_ref, 2)
    out_ref[...] = part_ref[...] + (TIME_STEP * DIFFUSION) * placed(sums, metric_ref[...], place_ref)


def land_second(
    in_other, in_far, part_ref, slot_ref, metric_ref, coef_in_ref, place_ref,
    out_ref,
    theirs_ref, zs_ref, left_ref,
):
    block = in_far.shape[0] // 2
    theirs_ref[0:block, :] = in_far[0:block, :]
    theirs_ref[block : 2 * block, :] = in_other[0:block, :]
    y = {(a, b): theirs_ref[pl.ds(6 * a + b, 4, stride=36), :] for a in range(6) for b in range(6)}
    sums = land(y, slot_ref[...], coef_in_ref, zs_ref, metric_ref.shape[1], left_ref, 2)
    out_ref[...] = part_ref[...] + (0.5 * TIME_STEP * DIFFUSION) * placed(sums, metric_ref[...], place_ref)


def known_rate(
    sums, faces_ref, counts, mates, metric, u, pin, rate_ref,
):
    elems = faces_ref.shape[1]
    metric2 = both_lanes(metric)
    lift = (LIFTING * metric2) * side_by_side(sums, elems)
    own = own_share(faces_ref, counts, mates, metric, elems)
    whole = 4 * 6 * PAD
    terms = jnp.concatenate([own[:whole], own[whole:] + lift, (metric2 * metric2) * u], axis=0)
    nodes = u.shape[0]
    high, low = split(terms)
    both = mm(rate_ref[...], high)
    return DIFFUSION * (both[:nodes] + both[nodes:] + mm(rate_ref[0:nodes, :], low)) - both_lanes(pin) * u


def own_share(faces_ref, counts, mates, metric, elems):
    rows = 6 * PAD
    value_w = (0.5 * PENALTY * LIFTING) * metric * (metric * counts + mates)
    deriv_w = (0.5 * LIFTING) * metric * counts

    def faces(kind, comp):
        at = (kind * 2 + comp) * rows
        return faces_ref[at : at + rows, :].astype(F32) + faces_ref[at + 4 * rows : at + 5 * rows, :].astype(F32)

    per_comp = []
    for comp in range(2):
        v, g = faces(0, comp), faces(1, comp)
        blocks = []
        for quarter in range(5):
            for f in range(6):
                at = slice(f * PAD, (f + 1) * PAD)
                row = slice(8 * f + quarter, 8 * f + quarter + 1)
                blocks.append(-(value_w[row] * v[at] + deriv_w[row] * g[at]))
        per_comp.append(jnp.concatenate(blocks, axis=0))
    return jnp.concatenate(per_comp, axis=1)


def placed(sums, metric, place_ref):
    high, low = split((LIFTING * both_lanes(metric)) * sums)
    place = place_ref[...]
    return mm(place, high) + mm(place, low)


def finish_first(
    in_swap, in_other, in_far, near_sent, far_sent, part_ref, slot_ref, metric_ref, coef_ref, coef_in_ref,
    place_ref, traces_ref,
    u1_ref, faces1_ref, mate_ref, near_ref, far_ref, other_ref,
    msg_ref, all_ref, own_ref, xs_ref, zs_ref, spread_ref, left_ref,
):
    elems = faces1_ref.shape[1]
    metric = metric_ref[...]
    slot_rows = slot_ref[...]
    arrived(in_swap, in_far, in_other, all_ref)
    block = near_sent.shape[0]
    own_ref[0:block, :] = near_sent[...]
    own_ref[block : 2 * block, :] = far_sent[block : 2 * block, :]
    own_m = spread(slot_rows, spread_ref)(5)
    mate_m = all_ref[pl.ds(72, 8, stride=FIRST), :]
    y = first_terms(all_ref, own_ref, own_m[0:4])
    sums = land(y, slot_rows, coef_in_ref, zs_ref, elems, left_ref, 0)
    mate_ref[...] = jnp.concatenate(
        [all_ref[s * block + 72 : s * block + 73, :] for s in range(CHANNELS)], axis=1
    )
    u1 = part_ref[...] + (TIME_STEP * DIFFUSION) * placed(sums, metric, place_ref)
    u1_ref[...] = u1
    face_tables_of(u1, both_lanes(metric), traces_ref[...], faces1_ref)
    sent = (near_ref, far_ref, other_ref)
    send_message(faces1_ref, slot_rows, coef_ref, xs_ref, spread_ref, msg_ref, sent, False, mate_m)


def local_second(
    near_ref, faces_ref, entry_ref, partner_ref, slot_ref, mate_ref, metric_ref, u0_ref, u_ref, pin_ref, counts_ref,
    coef_ref, rate_ref,
    near_out_ref, part_ref,
    xs_ref, zs_ref, spread_ref, left_ref,
):
    near_out_ref[...] = near_ref[...]
    elems = faces_ref.shape[1]
    sums = local_entries(
        faces_ref, entry_ref[...], partner_ref[...], coef_ref, xs_ref, zs_ref, spread_ref, left_ref
    )
    slot_rows = slot_ref[...]
    kinds = sub_iota((48, slot_rows.shape[1])) == as_int(8.0 * slot_rows[1:2] + slot_rows[2:3])
    high, low = split(jnp.where(kinds & (slot_rows[4:5] > 0.5), mate_ref[...], 0.0))
    hot = one_hot(as_int(slot_rows[0:1]), elems)
    mates = counts_ref[1] + mm_nt(high, hot) + mm_nt(low, hot)
    u = u_ref[...]
    rate = known_rate(
        sums, faces_ref, counts_ref[0], mates, metric_ref[...], u, pin_ref[...],
        rate_ref,
    )
    part_ref[...] = 0.5 * u0_ref[...] + 0.5 * (u + TIME_STEP * rate)


def finish_second(
    in_swap, part_ref, slot_ref, metric_ref, coef_in_ref, place_ref,
    out_ref,
    zs_ref, left_ref,
):
    elems = metric_ref.shape[1]
    y = {(a, b): in_swap[pl.ds(6 * a + b, 4, stride=36), :] for a in range(6) for b in range(6)}
    sums = land(y, slot_ref[...], coef_in_ref, zs_ref, elems, left_ref, 0)
    out = part_ref[...] + (0.5 * TIME_STEP * DIFFUSION) * placed(sums, metric_ref[...], place_ref)
    for comp in range(2):
        out_ref[comp] = out[:, comp * elems : (comp + 1) * elems]


def call(kernel, outs, scratch, *args, smem=0, copies=0):
    vmem = pl.BlockSpec(memory_space=pltpu.VMEM)
    scalar = pl.BlockSpec(memory_space=pltpu.SMEM)
    given = pl.BlockSpec(memory_space=pl.ANY) if copies else vmem
    scratch_shapes = [pltpu.VMEM(shape, dtype) for shape, dtype in scratch]
    if copies:
        scratch_shapes.append(pltpu.SemaphoreType.DMA((copies,)))
    return pl.pallas_call(
        kernel,
        out_shape=[jax.ShapeDtypeStruct(shape, dtype) for shape, dtype in outs],
        in_specs=[scalar] * smem + [given] * (len(args) - smem),
        out_specs=[vmem] * len(outs),
        scratch_shapes=scratch_shapes,
        compiler_params=pltpu.CompilerParams(vmem_limit_bytes=(53 if copies else 16) * 2**20),
        cost_estimate=pl.CostEstimate(flops=10**9, bytes_accessed=4000000, transcendentals=0),
    )(*args)


def pairings(count):
    near = [(i, i + 1) for i in range(0, count - 1, 2)]
    far = [(i, i + 2) for i in range(count - 2) if i & 2 == 0]
    other = [(i, i + 2) for i in range(count - 2) if i & 2]
    return [[*pairs, *((b, a) for a, b in pairs)] for pairs in (near, far, other)]


def cross_exchange(far, other):
    _, far_route, other_route = pairings(lax.axis_size("slab"))
    other = lax.ppermute(other, "slab", other_route)
    far = lax.ppermute(far, "slab", far_route)
    return far, other


def sibling_exchange(near, far, other):
    own = lax.axis_index("slab")
    rows = near.shape[0]
    from_other = ((own ^ (own >> 1)) & 1) == 1
    relayed = jnp.where(from_other, other[rows:], far[rows:])
    near_route = pairings(lax.axis_size("slab"))[0]
    return lax.ppermute(jnp.concatenate([near, relayed], axis=0), "slab", near_route)


def on_device(order_field, pinning, metric, elem_count, mortar_table):
    elems = order_field.shape[2]
    lanes = mortar_table.shape[1]
    own_id = lax.axis_index("slab").astype(I32).reshape(1)
    wide = 2 * elems
    rows = 6 * PAD
    slots = CHANNELS * CAP
    both = 2 * lanes // 128
    few = 2 * CHANNELS
    first_rows = few * FIRST
    second_rows = few * 36
    first_sent = [((n * first_rows // CHANNELS, 128), F32) for n in (1, 2, 2)]
    second_sent = [((n * second_rows // CHANNELS, 128), F32) for n in (1, 2, 2)]
    field_out = ((216, wide), F32)
    faces_out = ((8 * rows, elems), BF16)
    few_scratch = [((few * 2 * PAD, 128), F32), ((4 * PAD, 128), F32), ((few * 8, 128), F32), ((4 * rows, 2 * CAP), BF16)]
    both_scratch = [((both * 2 * PAD, 128), F32), ((both * PAD, 128), F32), ((both * 8, 128), F32), ((4 * rows, lanes), BF16)]
    traces, rate, place = (TABLES[name] for name in ("traces", "rate", "place"))
    metric_row, table, u0, slot, coef_out, near, far, other = call(
        prepare,
        [
            ((1, elems), F32), (mortar_table.shape, I32), field_out, ((8, slots), F32), ((73, few, 128), F32), *first_sent,
        ],
        [
            faces_out, ((first_rows, 128), F32), (order_field.shape, F32), (traces.shape, BF16),
            few_scratch[0], few_scratch[2],
        ],
        own_id, elem_count, mortar_table, metric.reshape(1, elems), order_field, traces,
        smem=2, copies=4,
    )
    got_far, got_other = cross_exchange(far, other)
    passed, part, entry, mates, counts, coef_local, coef_in = call(
        local_first,
        [
            first_sent[0], field_out, ((8, lanes), F32), ((8, lanes), F32), ((2, 48, elems), F32),
            ((73, both, 128), F32), ((73, few, 128), F32),
        ],
        [faces_out, *both_scratch],
        own_id, near, table, slot, metric_row, u0, pinning, traces, rate,
        smem=1,
    )
    got_swap = sibling_exchange(passed, got_far, got_other)
    (landed,) = call(
        land_first,
        [field_out],
        [((first_rows // 2, 128), F32), ((first_rows // 2, 128), F32), *few_scratch[1:]],
        got_other, got_far, far, other, part, slot, metric_row, coef_in, place,
    )
    u1, faces1, mate_row, near, far, other = call(
        finish_first,
        [field_out, faces_out, ((1, slots), F32), *second_sent],
        [((second_rows, 128), F32), ((first_rows, 128), F32), ((first_rows, 128), F32), *few_scratch],
        got_swap, got_other, got_far, near, far, landed, slot, metric_row, coef_out, coef_in,
        place, traces,
    )
    got_far, got_other = cross_exchange(far, other)
    passed, part = call(
        local_second,
        [second_sent[0], field_out],
        both_scratch,
        near, faces1, entry, mates, slot, mate_row, metric_row, u0, u1, pinning, counts, coef_local,
        rate,
    )
    got_swap = sibling_exchange(passed, got_far, got_other)
    (landed,) = call(
        land_second,
        [field_out],
        [((second_rows // 2, 128), F32), few_scratch[1], few_scratch[3]],
        got_other, got_far, part, slot, metric_row, coef_in, place,
    )
    (out,) = call(
        finish_second,
        [(order_field.shape, F32)],
        [few_scratch[1], few_scratch[3]],
        got_swap, landed, slot, metric_row, coef_in, place,
    )
    return out


def solution(mesh):
    split_all = ("groups", "slab")
    return jax.shard_map(
        on_device,
        mesh=mesh,
        in_specs=(
            P(None, None, split_all), P(None, split_all), P(split_all), P(split_all), P(None, split_all),
        ),
        out_specs=P(None, None, split_all),
        check_vma=False,
    )
```
